512 devices in a mesh: seq: 64 (over x, z_hi, y), head: 8 (over z_lo, core).
Axes of the slice: x: 4, y: 4, z: 16 (z_hi: 4, z_lo: 4; z = z_hi * 4 + z_lo), core: 2. Of those that a mesh axis runs over, the one named last changes fastest.
Arguments:
- tokens: bfloat16 [16384, 2048], P('seq'), may hold values from -16 to 16
- latents: bfloat16 [512, 2048], P(None, 'seq'), may hold values from -6 to 6
- w_query: bfloat16 [2048, 2048], P('seq', 'head'), may hold values from -0.125 to 0.125
- w_key: bfloat16 [2048, 2048], P(None, 'head'), may hold values from -0.125 to 0.125
- w_value: bfloat16 [2048, 2048], P(None, 'head'), may hold values from -0.125 to 0.125
- cotangent: bfloat16 [512, 2048], P(None, 'head'), may hold values from -384 to 384
Outputs:
- token_grad: bfloat16 [16384, 2048], P('seq', 'head')
- latent_grad: float32 [512, 2048], P(None, 'seq')
- query_weight_grad: float32 [2048, 2048], P('seq', 'head')
- key_weight_grad: float32 [2048, 2048], P('seq', 'head')
- value_weight_grad: float32 [2048, 2048], P('seq', 'head')
The draws below stay inside these ranges and needn't reach their ends.
All inputs are finite; a program needn't handle non-finite values.
Results may differ from the reference program's by a relative error of at most 0.015.
The reference program's roundings to bfloat16 on the way (of `query`, `score_grad` and `query_grad`) count: a program that leaves them out, or rounds other values in their place, can miss the bound.
Values may be sent and summed in bfloat16 or wider, within the bound.
No kernel may reach another device: no remote copies, remote signals or barrier semaphores. Data moves between devices by JAX's collectives and lax.ppermute only.
A program may use at most 64 MiB of HBM per device.

```python
import jax
import jax.numpy as jnp
from jax import lax

D = 2048
HEADS = 16
HEAD_DIM = 128
LATENTS = 512
TOKENS = 16384
HD = 2048


def spiked(result, stream_key, source, target, shards_of, factor):
    def block_of(axis_at):
        return (jnp.arange(result.shape[axis_at]) // (result.shape[axis_at] // shards_of)).reshape((-1,) + (1,) * (result.ndim - 1 - axis_at))

    near = jax.random.permutation(stream_key, shards_of)[block_of(target)]
    second = (block_of(target) + shards_of // 2) % shards_of
    return jnp.where((block_of(source) == near) | (block_of(source) == second), factor * result, result)


def block_levels(stream_key, shape, shards, least, high):
    def one(position, parts):
        heights = jax.random.uniform(jax.random.fold_in(jax.random.fold_in(stream_key, 6), position), (parts,), jnp.float32, least / len(shards), high / len(shards))
        return jnp.repeat(jnp.exp(heights), shape[position] // parts).reshape((-1,) + (1,) * (len(shape) - position - 1))

    loudness = one(*shards[0])
    for cut in shards[1:]:
        loudness = loudness * one(*cut)
    return loudness


def bell_draw(rng, extent, scale, limit, pieces=(), kind=jnp.bfloat16):
    entries = jax.random.normal(rng, extent, jnp.float32) * scale
    if len(pieces) > 0:
        entries = block_levels(rng, extent, pieces, -0.22, 0.18) * entries
    return jnp.clip(entries, min=-limit, max=limit).astype(kind)


def heavy_noise(key, shape, width, bound, split, heavy, held_as=jnp.bfloat16):
    values = width * jax.random.normal(key, shape, jnp.float32)
    if split:
        values = values * block_levels(key, shape, split, -0.22, 0.18)
    return jnp.clip(spiked(values, jax.random.fold_in(key, 3), *heavy), -bound, bound).astype(held_as)


def setup_inputs(seed: int = 0) -> dict:
    splits = jax.random.split(jax.random.key(seed), 7)
    return {
        "tokens": heavy_noise(splits[0], (TOKENS, D), 1.0, 16.0, ((0, 64),), (0, 1, 64, 4.0)),
        "latents": bell_draw(splits[1], (LATENTS, D), 1.0, 6.0, ((1, 64),)),
        "w_query": bell_draw(splits[2], (D, HD), D ** -0.5, 0.125, ((0, 64), (1, 8))),
        "w_key": bell_draw(splits[3], (D, HD), D ** -0.5, 0.125, ((1, 8),)),
        "w_value": bell_draw(splits[4], (D, HD), D ** -0.5, 0.125, ((1, 8),)),
        "cotangent": bell_draw(splits[5], (LATENTS, HD), (1 + TOKENS // 256), 384.0, ((1, 8),)),
    }


def reference(tokens, latents, w_query, w_key, w_value, cotangent):
    scale = HEAD_DIM ** -0.5
    query = jnp.dot(latents, w_query, preferred_element_type=jnp.float32).astype(jnp.bfloat16)
    keys = jnp.dot(tokens, w_key, preferred_element_type=jnp.float32).astype(jnp.bfloat16)
    values = jnp.dot(tokens, w_value, preferred_element_type=jnp.float32).astype(jnp.bfloat16)
    pos_t = jnp.arange(TOKENS, dtype=jnp.int32)
    pos_q = TOKENS - LATENTS + jnp.arange(LATENTS, dtype=jnp.int32)
    visible = pos_t[None, :] <= pos_q[:, None]

    def split_heads(array, count):
        return array.reshape(count, HEADS, HEAD_DIM).transpose(1, 0, 2)

    def per_head(items):
        q_h, k_h, v_h, c_h = items
        scores = jnp.dot(q_h, k_h.T, preferred_element_type=jnp.float32) * scale
        expo = jnp.where(visible, jnp.exp(scores), jnp.float32(0.0))
        denom = jnp.sum(expo, axis=1, keepdims=True)
        probs = expo / denom
        dprob = jnp.dot(c_h, v_h.T, preferred_element_type=jnp.float32)
        delta = jnp.sum(probs * dprob, axis=1, keepdims=True)
        score_grad = (probs * (dprob - delta) * scale).astype(jnp.bfloat16)
        dq_h = jnp.dot(score_grad, k_h, preferred_element_type=jnp.float32)
        dk_h = jnp.dot(score_grad.T, q_h, preferred_element_type=jnp.float32).astype(jnp.bfloat16)
        dv_h = jnp.dot(probs.astype(jnp.bfloat16).T, c_h, preferred_element_type=jnp.float32).astype(jnp.bfloat16)
        return dq_h, dk_h, dv_h

    dq_all, dk_all, dv_all = lax.map(per_head, (split_heads(query, LATENTS), split_heads(keys, TOKENS),
                                                split_heads(values, TOKENS), split_heads(cotangent, LATENTS)))
    query_grad = dq_all.transpose(1, 0, 2).reshape(LATENTS, HD).astype(jnp.bfloat16)
    key_grad = dk_all.transpose(1, 0, 2).reshape(TOKENS, HD)
    value_grad = dv_all.transpose(1, 0, 2).reshape(TOKENS, HD)
    token_grad = (jnp.dot(key_grad, w_key.T, preferred_element_type=jnp.float32)
                  + jnp.dot(value_grad, w_value.T, preferred_element_type=jnp.float32)).astype(jnp.bfloat16)
    key_weight_grad = jnp.dot(tokens.T, key_grad, preferred_element_type=jnp.float32)
    value_weight_grad = jnp.dot(tokens.T, value_grad, preferred_element_type=jnp.float32)
    query_weight_grad = jnp.dot(latents.T, query_grad, preferred_element_type=jnp.float32)
    latent_grad = jnp.dot(query_grad, w_query.T, preferred_element_type=jnp.float32)
    return token_grad, latent_grad, query_weight_grad, key_weight_grad, value_weight_grad
```

```python
import jax
import jax.numpy as jnp
from jax import lax
from jax.experimental import pallas as pl
from jax.experimental.pallas import tpu as pltpu
from jax.sharding import Mesh
from jax.sharding import PartitionSpec as P

HEAD_DIM = 128
SCALE = HEAD_DIM ** (-0.5)
SEQ = ("x", "w", "y")
HEAD = ("z", "c")
NEAR = ("x", "y")
F32 = jnp.float32
BF16 = jnp.bfloat16
SMEM = pl.BlockSpec(memory_space=pltpu.SMEM)
HBM = pl.BlockSpec(memory_space=pl.ANY)
NT = (((1,), (1,)), ((), ()))
MIB = 1024 * 1024
SHRINK = 2.0**-12


def dot(a, b):
    return jnp.dot(a, b, preferred_element_type=F32)


def dot_nt(a, b):
    return lax.dot_general(a, b, NT, preferred_element_type=F32)


def shape(dims, dtype):
    return jax.ShapeDtypeStruct(dims, dtype)


def whole(array):
    rank = len(array.shape)
    return pl.BlockSpec(array.shape, lambda i: (0,) * rank)


def local(body, outs, args, flops=0, specs=None, grid=1, out_specs=None, scratch=(), limit=16):
    specs = specs or {}
    moved = sum(a.size * a.dtype.itemsize for a in list(args) + list(outs))
    return pl.pallas_call(
        body,
        out_shape=outs,
        grid=(grid,),
        in_specs=[specs.get(i) or whole(a) for i, a in enumerate(args)],
        out_specs=out_specs or [whole(o) for o in outs],
        scratch_shapes=list(scratch),
        compiler_params=pltpu.CompilerParams(vmem_limit_bytes=limit * MIB),
        cost_estimate=pl.CostEstimate(flops=flops, bytes_accessed=moved, transcendentals=0),
    )(*args)


def exchange(blocks, axes):
    return lax.all_to_all(blocks, axes, split_axis=0, concat_axis=0, tiled=True)


def partner(value, axis, flip):
    size = lax.axis_size(axis)
    return lax.ppermute(value, axis, [(i, i ^ flip) for i in range(size)])


def summed(blocks):
    acc = blocks[0].astype(F32)
    for j in range(1, blocks.shape[0]):
        acc = acc + blocks[j].astype(F32)
    return acc


def sum_kernel(blocks, out):
    acc = summed(blocks).astype(out.dtype)
    for j in range(out.shape[0]):
        out[j] = acc


def sum_copies(blocks, count, dtype):
    (out,) = local(sum_kernel, [shape((count,) + blocks.shape[1:], dtype)], [blocks])
    return out


def total_kernel(blocks, out):
    out[...] = summed(blocks)


def query_kernel(w_query, latents_t, out):
    part = lax.dot_general(
        w_query[...], latents_t[...], (((0,), (0,)), ((), ())), preferred_element_type=F32
    )
    n, each, _ = out.shape
    for j in range(n):
        out[j] = part[j * each : (j + 1) * each]


def prepare_kernel(place, tokens, w_key, w_value, keys, keys_t, values, tokens_t, other_t, own_t):
    key = dot(tokens[...], w_key[...])
    keys[...] = key.astype(BF16)
    keys_t[...] = key.T.astype(BF16)
    values[...] = dot(tokens[...], w_value[...]).astype(BF16)
    for x in range(4):
        for w in range(4):
            at = (x * 4 + w) * 128
            slab = tokens[:, at : at + 128].T
            for y in range(4):
                tokens_t[x * 4 + y, w * 32 : (w + 1) * 32, :] = slab[y * 32 : (y + 1) * 32, :]
    z, c = place[2], place[3]
    hops, depth, cols = own_t.shape
    half = depth // 2
    for k in range(hops):
        for core, out in ((c, own_t), (1 - c, other_t)):
            rows = pl.ds(pl.multiple_of(((z ^ k) * 2 + core) * cols, cols), cols)
            out[k, :half, :] = w_key[rows, :].T
            out[k, half:, :] = w_value[rows, :].T


def expo_of(place, h, query_t, keys):
    rows, lats = keys.shape[0], query_t.shape[1]
    cols = slice(h * HEAD_DIM, (h + 1) * HEAD_DIM)
    pos_t = place[0] * rows + lax.broadcasted_iota(jnp.int32, (rows, lats), 0)
    pos_q = place[1] + lax.broadcasted_iota(jnp.int32, (rows, lats), 1)
    scores = dot(keys[:, cols], query_t[cols, :]) * SCALE
    return jnp.where(pos_t <= pos_q, jnp.exp(scores), 0.0)


def dprob_of(h, values, cot):
    cols = slice(h * HEAD_DIM, (h + 1) * HEAD_DIM)
    return dot_nt(values[:, cols], cot[:, cols])


def split(value):
    high = value.astype(BF16)
    return high, (value - high.astype(F32)).astype(BF16)


def dot_split(a, value):
    high, low = split(value)
    return dot(a, high) + dot(a, low)


def expo_kernel(place, query_t, keys, keys_t, values, cot, spread):
    heads = keys.shape[1] // HEAD_DIM
    n = spread.shape[0]
    each = keys.shape[1] // n
    per_head = n // heads
    sums = []
    for h in range(heads):
        cols = slice(h * HEAD_DIM, (h + 1) * HEAD_DIM)
        expo = expo_of(place, h, query_t, keys)
        weighted = expo * (dprob_of(h, values, cot) * SHRINK)
        sums.append(jnp.sum(expo, axis=0, keepdims=True))
        sums.append(jnp.sum(weighted, axis=0, keepdims=True))
        first = dot_split(keys_t[cols, :], weighted)
        second = dot_split(keys_t[cols, :], expo)
        for j in range(per_head):
            rows = slice(j * each, (j + 1) * each)
            spread[h * per_head + j, :each, :] = first[rows, :]
            spread[h * per_head + j, each : 2 * each, :] = second[rows, :]
    packed = jnp.concatenate(sums + sums, axis=0)
    for j in range(n):
        spread[j, 2 * each :, :] = packed


def grad_kernel(place, sums4, query_t, keys, values, cot, tokens_hbm, blocks, both, tokens_t, sem):
    fetch = pltpu.make_async_copy(tokens_hbm, tokens_t, sem)
    fetch.start()
    heads = keys.shape[1] // HEAD_DIM
    sums = summed(sums4)
    n, held, _ = blocks.shape
    depth = tokens_t.shape[1]
    each = held - depth
    denoms, deltas = [], []
    for h in range(heads):
        cols = slice(h * HEAD_DIM, (h + 1) * HEAD_DIM)
        at = 2 * each + 2 * h
        denom = sums[at : at + 1, :]
        shrunk = sums[at + 1 : at + 2, :] / denom
        delta = shrunk * (1.0 / SHRINK)
        denoms.append(denom)
        deltas.append(shrunk)
        probs = expo_of(place, h, query_t, keys) / denom
        grad = (probs * (dprob_of(h, values, cot) - delta) * SCALE).astype(BF16)
        both[:, cols] = dot_nt(grad, query_t[cols, :]).astype(BF16)
        value_cols = slice((heads + h) * HEAD_DIM, (heads + h + 1) * HEAD_DIM)
        both[:, value_cols] = dot(probs.astype(BF16), cot[:, cols]).astype(BF16)
    first_head = place[4] * heads < n
    denom = jnp.where(first_head, denoms[0], denoms[1])
    shrunk = jnp.where(first_head, deltas[0], deltas[1])
    query_grad = (sums[:each] - shrunk * sums[each : 2 * each]) / denom * (SCALE / SHRINK)
    query_grad = query_grad.astype(BF16)
    fetch.wait()
    tall = 4
    for j in range(0, n, tall):
        part = dot(tokens_t[j : j + tall].reshape(tall * depth, -1), both[...]).astype(BF16)
        for i in range(tall):
            blocks[j + i, :depth, :] = part[i * depth : (i + 1) * depth]
            blocks[j + i, depth:, :] = query_grad


def other_kernel(both, weights, other):
    for k in range(other.shape[0]):
        other[k] = dot(both[...], weights[k]).astype(BF16)


def pair_kernel(both, weights, other, here, *away):
    here[...] = dot(both[...], weights[0]) + other[0].astype(F32)
    for k, out in enumerate(away):
        out[...] = (dot(both[...], weights[k + 1]) + other[k + 1].astype(F32)).astype(BF16)


def token_sum_kernel(here, one, two, three, out):
    total = here[...] + one[...].astype(F32) + two[...].astype(F32) + three[...].astype(F32)
    out[...] = total.astype(BF16)


def near_sum_kernel(arrived, out):
    acc = summed(arrived)
    share = out.shape[1]
    for w in range(out.shape[0]):
        out[w] = acc[w * share : (w + 1) * share].astype(BF16)


def far_sum_kernel(arrived, key_weight, value_weight):
    width = key_weight.shape[1]
    acc = summed(arrived)
    key_weight[...] = acc[:, :width]
    value_weight[...] = acc[:, width:]


def on_device(tokens, latents, w_query, w_key, w_value, cotangent):
    rows, depth = tokens.shape
    lats = latents.shape[0]
    width = w_key.shape[1]
    heads = width // HEAD_DIM
    near, far = lax.axis_size(NEAR), lax.axis_size("w")
    n_seq = lax.axis_size(SEQ)
    n_head = lax.axis_size(HEAD)
    share = depth // n_seq
    each = width // near
    z, c = lax.axis_index("z"), lax.axis_index("c")
    place = jnp.stack([lax.axis_index(SEQ), rows * n_seq - lats, z, c, lax.axis_index(NEAR)])
    place = place.astype(jnp.int32)
    scalars = {0: SMEM}

    (query_part,) = local(
        query_kernel, [shape((near, each, lats), F32)], [w_query, latents.T], 2 * share * width * lats
    )
    query_part = exchange(query_part, NEAR)
    query_part = exchange(sum_copies(query_part, far, F32), "w")
    query_t = exchange(sum_copies(query_part, near, BF16), NEAR).reshape(width, lats)

    block = depth // n_head
    hops = n_head // 2
    keys, keys_t, values, tokens_t, other_t, own_t = local(
        prepare_kernel,
        [
            shape((rows, width), BF16),
            shape((width, rows), BF16),
            shape((rows, width), BF16),
            shape((near, depth // near, rows), BF16),
            shape((hops, 2 * width, block), BF16),
            shape((hops, 2 * width, block), BF16),
        ],
        [place, tokens, w_key, w_value],
        2 * rows * depth * 2 * width,
        specs=scalars,
        limit=60,
    )

    (spread,) = local(
        expo_kernel,
        [shape((near, 2 * each + 4 * heads, lats), F32)],
        [place, query_t, keys, keys_t, values, cotangent],
        12 * rows * width * lats,
        specs=scalars,
        limit=60,
    )
    sums = exchange(sum_copies(exchange(spread, NEAR), far, F32), "w")

    blocks, both = local(
        grad_kernel,
        [shape((near, depth // near + each, 2 * width), BF16), shape((rows, 2 * width), BF16)],
        [place, sums, query_t, keys, values, cotangent, tokens_t],
        8 * rows * width * lats + 2 * rows * depth * 2 * width,
        specs={0: SMEM, 6: HBM},
        scratch=[pltpu.VMEM(tokens_t.shape, BF16), pltpu.SemaphoreType.DMA(())],
        limit=60,
    )
    arrived = exchange(blocks, NEAR)

    (other,) = local(
        other_kernel,
        [shape((hops, rows, block), BF16)],
        [both, other_t],
        rows * depth * 2 * width,
        limit=60,
    )
    here, *away = local(
        pair_kernel,
        [shape((rows, block), F32)] + [shape((rows, block), BF16)] * (hops - 1),
        [both, own_t, partner(other, "c", 1)],
        rows * depth * 2 * width,
        limit=60,
    )
    parts = [partner(part, "z", k + 1) for k, part in enumerate(away)]
    arrived, here, *parts = lax.optimization_barrier((arrived, here, *parts))
    (token_grad,) = local(token_sum_kernel, [shape((rows, block), BF16)], [here, *parts], limit=60)

    query_grad_t = arrived[:, depth // near :, :].reshape(width, lats)
    latent_grad_t = dot(w_query, query_grad_t)
    query_weight_grad = lax.dot_general(
        latents, query_grad_t, (((0,), (1,)), ((), ())), preferred_element_type=F32
    )
    (sent,) = local(
        near_sum_kernel,
        [shape((far, share, 2 * width), BF16)],
        [arrived],
        specs={0: pl.BlockSpec((near, depth // near, 2 * width), lambda i: (0, 0, 0))},
    )
    key_weight_grad, value_weight_grad = local(
        far_sum_kernel, [shape((share, width), F32)] * 2, [exchange(sent, "w")]
    )
    for axis, flip in (("c", 1), ("z", 1), ("z", 2)):
        latent_grad_t = latent_grad_t + partner(latent_grad_t, axis, flip)
    return (
        token_grad,
        latent_grad_t.T,
        query_weight_grad,
        key_weight_grad,
        value_weight_grad,
    )


def solution(mesh):
    fine = Mesh(mesh.devices.reshape(4, 4, 4, 4, 2), ("x", "w", "y", "z", "c"))
    placed = (
        P(SEQ, None),
        P(None, SEQ),
        P(SEQ, HEAD),
        P(None, HEAD),
        P(None, HEAD),
        P(None, HEAD),
    )
    return jax.shard_map(
        on_device,
        mesh=fine,
        in_specs=placed,
        out_specs=(
            P(SEQ, HEAD),
            P(None, SEQ),
            P(SEQ, HEAD),
            P(SEQ, HEAD),
            P(SEQ, HEAD),
        ),
        check_vma=False,
    )
```

```python
import jax
import jax.numpy as jnp
from jax import lax
from jax.experimental import pallas as pl
from jax.experimental.pallas import tpu as pltpu
from jax.sharding import Mesh
from jax.sharding import PartitionSpec as P

HEAD_DIM = 128
SCALE = HEAD_DIM ** (-0.5)
SEQ = ("x", "w", "y")
HEAD = ("z", "c")
NEAR = ("x", "y")
F32 = jnp.float32
BF16 = jnp.bfloat16
SMEM = pl.BlockSpec(memory_space=pltpu.SMEM)
HBM = pl.BlockSpec(memory_space=pl.ANY)
NT = (((1,), (1,)), ((), ()))
MIB = 1024 * 1024
SHRINK = 2.0**-12


def dot(a, b):
    return jnp.dot(a, b, preferred_element_type=F32)


def dot_nt(a, b):
    return lax.dot_general(a, b, NT, preferred_element_type=F32)


def shape(dims, dtype):
    return jax.ShapeDtypeStruct(dims, dtype)


def whole(array):
    rank = len(array.shape)
    return pl.BlockSpec(array.shape, lambda i: (0,) * rank)


def local(body, outs, args, flops=0, specs=None, grid=1, out_specs=None, scratch=(), limit=16):
    specs = specs or {}
    moved = sum(a.size * a.dtype.itemsize for a in list(args) + list(outs))
    return pl.pallas_call(
        body,
        out_shape=outs,
        grid=(grid,),
        in_specs=[specs.get(i) or whole(a) for i, a in enumerate(args)],
        out_specs=out_specs or [whole(o) for o in outs],
        scratch_shapes=list(scratch),
        compiler_params=pltpu.CompilerParams(vmem_limit_bytes=limit * MIB),
        cost_estimate=pl.CostEstimate(flops=flops, bytes_accessed=moved, transcendentals=0),
    )(*args)


def exchange(blocks, axes):
    return lax.all_to_all(blocks, axes, split_axis=0, concat_axis=0, tiled=True)


def partner(value, axis, flip):
    size = lax.axis_size(axis)
    return lax.ppermute(value, axis, [(i, i ^ flip) for i in range(size)])


def summed(blocks):
    acc = blocks[0].astype(F32)
    for j in range(1, blocks.shape[0]):
        acc = acc + blocks[j].astype(F32)
    return acc


def sum_kernel(blocks, out):
    acc = summed(blocks).astype(out.dtype)
    for j in range(out.shape[0]):
        out[j] = acc


def sum_copies(blocks, count, dtype):
    (out,) = local(sum_kernel, [shape((count,) + blocks.shape[1:], dtype)], [blocks])
    return out


def total_kernel(blocks, out):
    out[...] = summed(blocks)


def query_kernel(w_query, latents_t, out):
    part = lax.dot_general(
        w_query[...], latents_t[...], (((0,), (0,)), ((), ())), preferred_element_type=F32
    )
    n, each, _ = out.shape
    for j in range(n):
        out[j] = part[j * each : (j + 1) * each]


def prepare_kernel(place, tokens, w_key, w_value, keys, keys_t, values, tokens_t, other_t, own_t):
    key = dot(tokens[...], w_key[...])
    keys[...] = key.astype(BF16)
    keys_t[...] = key.T.astype(BF16)
    values[...] = dot(tokens[...], w_value[...]).astype(BF16)
    for x in range(4):
        for w in range(4):
            at = (x * 4 + w) * 128
            slab = tokens[:, at : at + 128].T
            for y in range(4):
                tokens_t[x * 4 + y, w * 32 : (w + 1) * 32, :] = slab[y * 32 : (y + 1) * 32, :]
    z, c = place[2], place[3]
    hops, depth, cols = own_t.shape
    half = depth // 2
    for k in range(hops):
        for core, out in ((c, own_t), (1 - c, other_t)):
            rows = pl.ds(pl.multiple_of(((z ^ k) * 2 + core) * cols, cols), cols)
            out[k, :half, :] = w_key[rows, :].T
            out[k, half:, :] = w_value[rows, :].T


def expo_of(place, h, query_t, keys):
    rows, lats = keys.shape[0], query_t.shape[1]
    cols = slice(h * HEAD_DIM, (h + 1) * HEAD_DIM)
    pos_t = place[0] * rows + lax.broadcasted_iota(jnp.int32, (rows, lats), 0)
    pos_q = place[1] + lax.broadcasted_iota(jnp.int32, (rows, lats), 1)
    scores = dot(keys[:, cols], query_t[cols, :]) * SCALE
    return jnp.where(pos_t <= pos_q, jnp.exp(scores), 0.0)


def dprob_of(h, values, cot):
    cols = slice(h * HEAD_DIM, (h + 1) * HEAD_DIM)
    return dot_nt(values[:, cols], cot[:, cols])


def split(value):
    high = value.astype(BF16)
    return high, (value - high.astype(F32)).astype(BF16)


def dot_split(a, value):
    high, low = split(value)
    return dot(a, high) + dot(a, low)


def expo_kernel(place, query_t, keys, keys_t, values, cot, spread):
    heads = keys.shape[1] // HEAD_DIM
    n = spread.shape[0]
    each = keys.shape[1] // n
    per_head = n // heads
    sums = []
    for h in range(heads):
        cols = slice(h * HEAD_DIM, (h + 1) * HEAD_DIM)
        expo = expo_of(place, h, query_t, keys)
        weighted = expo * (dprob_of(h, values, cot) * SHRINK)
        sums.append(jnp.sum(expo, axis=0, keepdims=True))
        sums.append(jnp.sum(weighted, axis=0, keepdims=True))
        first = dot_split(keys_t[cols, :], weighted)
        second = dot_split(keys_t[cols, :], expo)
        for j in range(per_head):
            rows = slice(j * each, (j + 1) * each)
            spread[h * per_head + j, :each, :] = first[rows, :]
            spread[h * per_head + j, each : 2 * each, :] = second[rows, :]
    packed = jnp.concatenate(sums + sums, axis=0)
    for j in range(n):
        spread[j, 2 * each :, :] = packed


def grad_kernel(
    place, sums4, query_t, keys, values, cot, tokens_hbm, other_hbm, blocks, both, other, tokens_t, other_t, sems
):
    fetch = pltpu.make_async_copy(tokens_hbm, tokens_t, sems.at[0])
    fetch_other = pltpu.make_async_copy(other_hbm, other_t, sems.at[1])
    fetch.start()
    fetch_other.start()
    heads = keys.shape[1] // HEAD_DIM
    sums = summed(sums4)
    n, held, _ = blocks.shape
    depth = tokens_t.shape[1]
    each = held - depth
    denoms, deltas = [], []
    for h in range(heads):
        cols = slice(h * HEAD_DIM, (h + 1) * HEAD_DIM)
        at = 2 * each + 2 * h
        denom = sums[at : at + 1, :]
        shrunk = sums[at + 1 : at + 2, :] / denom
        delta = shrunk * (1.0 / SHRINK)
        denoms.append(denom)
        deltas.append(shrunk)
        probs = expo_of(place, h, query_t, keys) / denom
        grad = (probs * (dprob_of(h, values, cot) - delta) * SCALE).astype(BF16)
        both[:, cols] = dot_nt(grad, query_t[cols, :]).astype(BF16)
        value_cols = slice((heads + h) * HEAD_DIM, (heads + h + 1) * HEAD_DIM)
        both[:, value_cols] = dot(probs.astype(BF16), cot[:, cols]).astype(BF16)
    first_head = place[4] * heads < n
    denom = jnp.where(first_head, denoms[0], denoms[1])
    shrunk = jnp.where(first_head, deltas[0], deltas[1])
    query_grad = (sums[:each] - shrunk * sums[each : 2 * each]) / denom * (SCALE / SHRINK)
    query_grad = query_grad.astype(BF16)
    fetch.wait()
    tall = 4
    for j in range(0, n, tall):
        part = dot(tokens_t[j : j + tall].reshape(tall * depth, -1), both[...]).astype(BF16)
        for i in range(tall):
            blocks[j + i, :depth, :] = part[i * depth : (i + 1) * depth]
            blocks[j + i, depth:, :] = query_grad
    fetch_other.wait()
    for k in range(other.shape[0]):
        other[k] = dot(both[...], other_t[k]).astype(BF16)


def pair_kernel(both, weights, other, here, *away):
    here[...] = dot(both[...], weights[0]) + other[0].astype(F32)
    for k, out in enumerate(away):
        out[...] = (dot(both[...], weights[k + 1]) + other[k + 1].astype(F32)).astype(BF16)


def token_sum_kernel(here, one, two, three, out):
    total = here[...] + one[...].astype(F32) + two[...].astype(F32) + three[...].astype(F32)
    out[...] = total.astype(BF16)


def near_sum_kernel(arrived, out):
    acc = summed(arrived)
    share = out.shape[1]
    for w in range(out.shape[0]):
        out[w] = acc[w * share : (w + 1) * share].astype(BF16)


def far_sum_kernel(arrived, key_weight, value_weight):
    width = key_weight.shape[1]
    acc = summed(arrived)
    key_weight[...] = acc[:, :width]
    value_weight[...] = acc[:, width:]


def on_device(tokens, latents, w_query, w_key, w_value, cotangent):
    rows, depth = tokens.shape
    lats = latents.shape[0]
    width = w_key.shape[1]
    heads = width // HEAD_DIM
    near, far = lax.axis_size(NEAR), lax.axis_size("w")
    n_seq = lax.axis_size(SEQ)
    n_head = lax.axis_size(HEAD)
    share = depth // n_seq
    each = width // near
    z, c = lax.axis_index("z"), lax.axis_index("c")
    place = jnp.stack([lax.axis_index(SEQ), rows * n_seq - lats, z, c, lax.axis_index(NEAR)])
    place = place.astype(jnp.int32)
    scalars = {0: SMEM}

    (query_part,) = local(
        query_kernel, [shape((near, each, lats), F32)], [w_query, latents.T], 2 * share * width * lats, limit=60
    )
    query_part = exchange(query_part, NEAR)
    query_part = exchange(sum_copies(query_part, far, F32), "w")
    query_t = exchange(sum_copies(query_part, near, BF16), NEAR).reshape(width, lats)

    block = depth // n_head
    hops = n_head // 2
    keys, keys_t, values, tokens_t, other_t, own_t = local(
        prepare_kernel,
        [
            shape((rows, width), BF16),
            shape((width, rows), BF16),
            shape((rows, width), BF16),
            shape((near, depth // near, rows), BF16),
            shape((hops, 2 * width, block), BF16),
            shape((hops, 2 * width, block), BF16),
        ],
        [place, tokens, w_key, w_value],
        2 * rows * depth * 2 * width,
        specs=scalars,
        limit=60,
    )

    (spread,) = local(
        expo_kernel,
        [shape((near, 2 * each + 4 * heads, lats), F32)],
        [place, query_t, keys, keys_t, values, cotangent],
        12 * rows * width * lats,
        specs=scalars,
        limit=60,
    )
    sums = exchange(sum_copies(exchange(spread, NEAR), far, F32), "w")

    blocks, both, other = local(
        grad_kernel,
        [
            shape((near, depth // near + each, 2 * width), BF16),
            shape((rows, 2 * width), BF16),
            shape((hops, rows, block), BF16),
        ],
        [place, sums, query_t, keys, values, cotangent, tokens_t, other_t],
        8 * rows * width * lats + 3 * rows * depth * 2 * width,
        specs={0: SMEM, 6: HBM, 7: HBM},
        scratch=[
            pltpu.VMEM(tokens_t.shape, BF16),
            pltpu.VMEM(other_t.shape, BF16),
            pltpu.SemaphoreType.DMA((2,)),
        ],
        limit=60,
    )
    arrived = exchange(blocks, NEAR)

    here, *away = local(
        pair_kernel,
        [shape((rows, block), F32)] + [shape((rows, block), BF16)] * (hops - 1),
        [both, own_t, partner(other, "c", 1)],
        rows * depth * 2 * width,
        limit=60,
    )
    parts = [partner(away[k - 1], "z", k) for k in (2, 3, 1)]
    arrived, here, *parts = lax.optimization_barrier((arrived, here, *parts))
    (token_grad,) = local(token_sum_kernel, [shape((rows, block), BF16)], [here, *parts], limit=60)

    (sent,) = local(
        near_sum_kernel,
        [shape((far, share, 2 * width), BF16)],
        [arrived],
        specs={0: pl.BlockSpec((near, depth // near, 2 * width), lambda i: (0, 0, 0))},
    )
    query_grad_t = arrived[:, depth // near :, :].reshape(width, lats)
    sent, query_grad_t = lax.optimization_barrier((sent, query_grad_t))
    key_weight_grad, value_weight_grad = local(
        far_sum_kernel, [shape((share, width), F32)] * 2, [exchange(sent, "w")]
    )
    latent_grad_t = dot(w_query, query_grad_t)
    query_weight_grad = lax.dot_general(
        latents, query_grad_t, (((0,), (1,)), ((), ())), preferred_element_type=F32
    )
    for axis, flip in (("c", 1), ("z", 1), ("z", 2)):
        held = latent_grad_t.astype(BF16)
        latent_grad_t = held.astype(F32) + partner(held, axis, flip).astype(F32)
    return (
        token_grad,
        latent_grad_t.T,
        query_weight_grad,
        key_weight_grad,
        value_weight_grad,
    )


def solution(mesh):
    fine = Mesh(mesh.devices.reshape(4, 4, 4, 4, 2), ("x", "w", "y", "z", "c"))
    placed = (
        P(SEQ, None),
        P(None, SEQ),
        P(SEQ, HEAD),
        P(None, HEAD),
        P(None, HEAD),
        P(None, HEAD),
    )
    return jax.shard_map(
        on_device,
        mesh=fine,
        in_specs=placed,
        out_specs=(
            P(SEQ, HEAD),
            P(None, SEQ),
            P(SEQ, HEAD),
            P(SEQ, HEAD),
            P(SEQ, HEAD),
        ),
        check_vma=False,
    )
```

```python
import jax
import jax.numpy as jnp
from jax import lax
from jax.experimental import pallas as pl
from jax.experimental.pallas import tpu as pltpu
from jax.sharding import Mesh
from jax.sharding import PartitionSpec as P

HEAD_DIM = 128
SCALE = HEAD_DIM ** (-0.5)
SEQ = ("x", "w", "y")
HEAD = ("z", "c")
NEAR = ("x", "y")
F32 = jnp.float32
BF16 = jnp.bfloat16
SMEM = pl.BlockSpec(memory_space=pltpu.SMEM)
HBM = pl.BlockSpec(memory_space=pl.ANY)
NT = (((1,), (1,)), ((), ()))
MIB = 1024 * 1024
SHRINK = 2.0**-12


def dot(a, b):
    return jnp.dot(a, b, preferred_element_type=F32)


def dot_nt(a, b):
    return lax.dot_general(a, b, NT, preferred_element_type=F32)


def shape(dims, dtype):
    return jax.ShapeDtypeStruct(dims, dtype)


def whole(array):
    rank = len(array.shape)
    return pl.BlockSpec(array.shape, lambda i: (0,) * rank)


def local(body, outs, args, flops=0, specs=None, grid=1, out_specs=None, scratch=(), limit=16):
    specs = specs or {}
    moved = sum(a.size * a.dtype.itemsize for a in list(args) + list(outs))
    return pl.pallas_call(
        body,
        out_shape=outs,
        grid=(grid,),
        in_specs=[specs.get(i) or whole(a) for i, a in enumerate(args)],
        out_specs=out_specs or [whole(o) for o in outs],
        scratch_shapes=list(scratch),
        compiler_params=pltpu.CompilerParams(vmem_limit_bytes=limit * MIB),
        cost_estimate=pl.CostEstimate(flops=flops, bytes_accessed=moved, transcendentals=0),
    )(*args)


def exchange(blocks, axes):
    return lax.all_to_all(blocks, axes, split_axis=0, concat_axis=0, tiled=True)


def partner(value, axis, flip):
    size = lax.axis_size(axis)
    return lax.ppermute(value, axis, [(i, i ^ flip) for i in range(size)])


def summed(blocks):
    acc = blocks[0].astype(F32)
    for j in range(1, blocks.shape[0]):
        acc = acc + blocks[j].astype(F32)
    return acc


def sum_kernel(blocks, out):
    acc = summed(blocks).astype(out.dtype)
    for j in range(out.shape[0]):
        out[j] = acc


def sum_copies(blocks, count, dtype):
    (out,) = local(sum_kernel, [shape((count,) + blocks.shape[1:], dtype)], [blocks])
    return out


def total_kernel(blocks, out):
    out[...] = summed(blocks)


def query_kernel(w_query, latents_t, out):
    part = lax.dot_general(
        w_query[...], latents_t[...], (((0,), (0,)), ((), ())), preferred_element_type=F32
    )
    n, each, _ = out.shape
    for j in range(n):
        out[j] = part[j * each : (j + 1) * each]


def prepare_kernel(place, tokens, w_key, w_value, keys, keys_t, values, tokens_t, other_t, own_t):
    key = dot(tokens[...], w_key[...])
    keys[...] = key.astype(BF16)
    keys_t[...] = key.T.astype(BF16)
    values[...] = dot(tokens[...], w_value[...]).astype(BF16)
    for x in range(4):
        for w in range(4):
            at = (x * 4 + w) * 128
            slab = tokens[:, at : at + 128].T
            for y in range(4):
                tokens_t[x * 4 + y, w * 32 : (w + 1) * 32, :] = slab[y * 32 : (y + 1) * 32, :]
    z, c = place[2], place[3]
    hops, depth, cols = own_t.shape
    half = depth // 2
    for k in range(hops):
        for core, out in ((c, own_t), (1 - c, other_t)):
            rows = pl.ds(pl.multiple_of(((z ^ k) * 2 + core) * cols, cols), cols)
            out[k, :half, :] = w_key[rows, :].T
            out[k, half:, :] = w_value[rows, :].T


def expo_of(place, h, query_t, keys):
    rows, lats = keys.shape[0], query_t.shape[1]
    cols = slice(h * HEAD_DIM, (h + 1) * HEAD_DIM)
    pos_t = place[0] * rows + lax.broadcasted_iota(jnp.int32, (rows, lats), 0)
    pos_q = place[1] + lax.broadcasted_iota(jnp.int32, (rows, lats), 1)
    scores = dot(keys[:, cols], query_t[cols, :]) * SCALE
    return jnp.where(pos_t <= pos_q, jnp.exp(scores), 0.0)


def dprob_of(h, values, cot):
    cols = slice(h * HEAD_DIM, (h + 1) * HEAD_DIM)
    return dot_nt(values[:, cols], cot[:, cols])


def split(value):
    high = value.astype(BF16)
    return high, (value - high.astype(F32)).astype(BF16)


def dot_split(a, value):
    high, low = split(value)
    return dot(a, high) + dot(a, low)


def expo_kernel(place, query_t, keys, keys_t, values, cot, spread):
    heads = keys.shape[1] // HEAD_DIM
    n = spread.shape[0]
    each = keys.shape[1] // n
    per_head = n // heads
    sums = []
    for h in range(heads):
        cols = slice(h * HEAD_DIM, (h + 1) * HEAD_DIM)
        expo = expo_of(place, h, query_t, keys)
        weighted = expo * (dprob_of(h, values, cot) * SHRINK)
        sums.append(jnp.sum(expo, axis=0, keepdims=True))
        sums.append(jnp.sum(weighted, axis=0, keepdims=True))
        first = dot_split(keys_t[cols, :], weighted)
        second = dot_split(keys_t[cols, :], expo)
        for j in range(per_head):
            rows = slice(j * each, (j + 1) * each)
            spread[h * per_head + j, :each, :] = first[rows, :]
            spread[h * per_head + j, each : 2 * each, :] = second[rows, :]
    packed = jnp.concatenate(sums + sums, axis=0)
    for j in range(n):
        spread[j, 2 * each :, :] = packed


def grad_kernel(
    place, sums4, query_t, keys, values, cot, tokens_hbm, other_hbm, blocks_hbm, both, other_out, *scratch
):
    tokens_t, other_t, blocks, other, sems = scratch
    fetch = pltpu.make_async_copy(tokens_hbm, tokens_t, sems.at[0])
    fetch_other = pltpu.make_async_copy(other_hbm, other_t, sems.at[1])
    fetch.start()
    fetch_other.start()
    heads = keys.shape[1] // HEAD_DIM
    sums = summed(sums4)
    n, rows, _ = blocks.shape
    depth = tokens_t.shape[1]
    each = rows - depth
    denoms, deltas = [], []
    for h in range(heads):
        cols = slice(h * HEAD_DIM, (h + 1) * HEAD_DIM)
        at = 2 * each + 2 * h
        denom = sums[at : at + 1, :]
        shrunk = sums[at + 1 : at + 2, :] / denom
        delta = shrunk * (1.0 / SHRINK)
        denoms.append(denom)
        deltas.append(shrunk)
        probs = expo_of(place, h, query_t, keys) / denom
        grad = (probs * (dprob_of(h, values, cot) - delta) * SCALE).astype(BF16)
        both[:, cols] = dot_nt(grad, query_t[cols, :]).astype(BF16)
        value_cols = slice((heads + h) * HEAD_DIM, (heads + h + 1) * HEAD_DIM)
        both[:, value_cols] = dot(probs.astype(BF16), cot[:, cols]).astype(BF16)
    first_head = place[4] * heads < n
    denom = jnp.where(first_head, denoms[0], denoms[1])
    shrunk = jnp.where(first_head, deltas[0], deltas[1])
    query_grad = (sums[:each] - shrunk * sums[each : 2 * each]) / denom * (SCALE / SHRINK)
    query_grad = query_grad.astype(BF16)
    fetch.wait()
    tall = 4
    leaving = []
    for j in range(0, n, tall):
        part = dot(tokens_t[j : j + tall].reshape(tall * depth, -1), both[...]).astype(BF16)
        for i in range(tall):
            blocks[j + i, :depth, :] = part[i * depth : (i + 1) * depth]
            blocks[j + i, depth:, :] = query_grad
        group = pl.ds(j, tall)
        leaving.append(
            pltpu.make_async_copy(blocks.at[group], blocks_hbm.at[group], sems.at[2 + j // tall])
        )
        leaving[-1].start()
    fetch_other.wait()
    for k in range(other.shape[0]):
        other[k] = dot(both[...], other_t[k]).astype(BF16)
    leaving.append(pltpu.make_async_copy(other, other_out, sems.at[2 + n // tall]))
    leaving[-1].start()
    for copy in leaving:
        copy.wait()


def pair_kernel(both, weights, other, here, *away):
    here[...] = dot(both[...], weights[0]) + other[0].astype(F32)
    for k, out in enumerate(away):
        out[...] = (dot(both[...], weights[k + 1]) + other[k + 1].astype(F32)).astype(BF16)


def token_sum_kernel(here, one, two, three, out):
    total = here[...] + one[...].astype(F32) + two[...].astype(F32) + three[...].astype(F32)
    out[...] = total.astype(BF16)


def near_sum_kernel(arrived, out):
    acc = summed(arrived)
    share = out.shape[1]
    for w in range(out.shape[0]):
        out[w] = acc[w * share : (w + 1) * share].astype(BF16)


def far_sum_kernel(arrived, key_weight, value_weight):
    width = key_weight.shape[1]
    acc = summed(arrived)
    key_weight[...] = acc[:, :width]
    value_weight[...] = acc[:, width:]


def on_device(tokens, latents, w_query, w_key, w_value, cotangent):
    rows, depth = tokens.shape
    lats = latents.shape[0]
    width = w_key.shape[1]
    heads = width // HEAD_DIM
    near, far = lax.axis_size(NEAR), lax.axis_size("w")
    n_seq = lax.axis_size(SEQ)
    n_head = lax.axis_size(HEAD)
    share = depth // n_seq
    each = width // near
    z, c = lax.axis_index("z"), lax.axis_index("c")
    place = jnp.stack([lax.axis_index(SEQ), rows * n_seq - lats, z, c, lax.axis_index(NEAR)])
    place = place.astype(jnp.int32)
    scalars = {0: SMEM}

    (query_part,) = local(
        query_kernel, [shape((near, each, lats), F32)], [w_query, latents.T], 2 * share * width * lats, limit=60
    )
    query_part = exchange(query_part, NEAR)
    query_part = exchange(sum_copies(query_part, far, F32), "w")
    query_t = exchange(sum_copies(query_part, near, BF16), NEAR).reshape(width, lats)

    block = depth // n_head
    hops = n_head // 2
    keys, keys_t, values, tokens_t, other_t, own_t = local(
        prepare_kernel,
        [
            shape((rows, width), BF16),
            shape((width, rows), BF16),
            shape((rows, width), BF16),
            shape((near, depth // near, rows), BF16),
            shape((hops, 2 * width, block), BF16),
            shape((hops, 2 * width, block), BF16),
        ],
        [place, tokens, w_key, w_value],
        2 * rows * depth * 2 * width,
        specs=scalars,
        limit=60,
    )

    (spread,) = local(
        expo_kernel,
        [shape((near, 2 * each + 4 * heads, lats), F32)],
        [place, query_t, keys, keys_t, values, cotangent],
        12 * rows * width * lats,
        specs=scalars,
        limit=60,
    )
    sums = exchange(sum_copies(exchange(spread, NEAR), far, F32), "w")

    blocks, both, other = local(
        grad_kernel,
        [
            shape((near, depth // near + each, 2 * width), BF16),
            shape((rows, 2 * width), BF16),
            shape((hops, rows, block), BF16),
        ],
        [place, sums, query_t, keys, values, cotangent, tokens_t, other_t],
        8 * rows * width * lats + 3 * rows * depth * 2 * width,
        specs={0: SMEM, 6: HBM, 7: HBM},
        scratch=[
            pltpu.VMEM(tokens_t.shape, BF16),
            pltpu.VMEM(other_t.shape, BF16),
            pltpu.VMEM((near, depth // near + each, 2 * width), BF16),
            pltpu.VMEM((hops, rows, block), BF16),
            pltpu.SemaphoreType.DMA((7,)),
        ],
        out_specs=[HBM, whole(shape((rows, 2 * width), BF16)), HBM],
        limit=60,
    )
    arrived = exchange(blocks, NEAR)

    here, *away = local(
        pair_kernel,
        [shape((rows, block), F32)] + [shape((rows, block), BF16)] * (hops - 1),
        [both, own_t, partner(other, "c", 1)],
        rows * depth * 2 * width,
        limit=60,
    )
    parts = [partner(away[k - 1], "z", k) for k in (2, 3, 1)]
    (token_grad,) = local(token_sum_kernel, [shape((rows, block), BF16)], [here, *parts], limit=60)
    arrived, token_grad = lax.optimization_barrier((arrived, token_grad))

    (sent,) = local(
        near_sum_kernel,
        [shape((far, share, 2 * width), BF16)],
        [arrived],
        specs={0: pl.BlockSpec((near, depth // near, 2 * width), lambda i: (0, 0, 0))},
    )
    query_grad_t = arrived[:, depth // near :, :].reshape(width, lats)
    sent, query_grad_t = lax.optimization_barrier((sent, query_grad_t))
    key_weight_grad, value_weight_grad = local(
        far_sum_kernel, [shape((share, width), F32)] * 2, [exchange(sent, "w")]
    )
    latent_grad_t = dot(w_query, query_grad_t)
    query_weight_grad = lax.dot_general(
        latents, query_grad_t, (((0,), (1,)), ((), ())), preferred_element_type=F32
    )
    for axis, flip in (("c", 1), ("z", 1), ("z", 2)):
        held = latent_grad_t.astype(BF16)
        latent_grad_t = held.astype(F32) + partner(held, axis, flip).astype(F32)
    return (
        token_grad,
        latent_grad_t.T,
        query_weight_grad,
        key_weight_grad,
        value_weight_grad,
    )


def solution(mesh):
    fine = Mesh(mesh.devices.reshape(4, 4, 4, 4, 2), ("x", "w", "y", "z", "c"))
    placed = (
        P(SEQ, None),
        P(None, SEQ),
        P(SEQ, HEAD),
        P(None, HEAD),
        P(None, HEAD),
        P(None, HEAD),
    )
    return jax.shard_map(
        on_device,
        mesh=fine,
        in_specs=placed,
        out_specs=(
            P(SEQ, HEAD),
            P(None, SEQ),
            P(SEQ, HEAD),
            P(SEQ, HEAD),
            P(SEQ, HEAD),
        ),
        check_vma=False,
    )
```

```python
import jax
import jax.numpy as jnp
from jax import lax
from jax.experimental import pallas as pl
from jax.experimental.pallas import tpu as pltpu
from jax.sharding import Mesh
from jax.sharding import PartitionSpec as P

HEAD_DIM = 128
SCALE = HEAD_DIM ** (-0.5)
SEQ = ("x", "w", "y")
HEAD = ("z", "c")
NEAR = ("x", "y")
F32 = jnp.float32
BF16 = jnp.bfloat16
SMEM = pl.BlockSpec(memory_space=pltpu.SMEM)
HBM = pl.BlockSpec(memory_space=pl.ANY)
NT = (((1,), (1,)), ((), ()))
MIB = 1024 * 1024
SHRINK = 2.0**-12


def dot(a, b):
    return jnp.dot(a, b, preferred_element_type=F32)


def dot_nt(a, b):
    return lax.dot_general(a, b, NT, preferred_element_type=F32)


def shape(dims, dtype):
    return jax.ShapeDtypeStruct(dims, dtype)


def whole(array):
    rank = len(array.shape)
    return pl.BlockSpec(array.shape, lambda i: (0,) * rank)


def local(body, outs, args, flops=0, specs=None, grid=1, out_specs=None, scratch=(), limit=16):
    specs = specs or {}
    moved = sum(a.size * a.dtype.itemsize for a in list(args) + list(outs))
    return pl.pallas_call(
        body,
        out_shape=outs,
        grid=(grid,),
        in_specs=[specs.get(i) or whole(a) for i, a in enumerate(args)],
        out_specs=out_specs or [whole(o) for o in outs],
        scratch_shapes=list(scratch),
        compiler_params=pltpu.CompilerParams(vmem_limit_bytes=limit * MIB),
        cost_estimate=pl.CostEstimate(flops=flops, bytes_accessed=moved, transcendentals=0),
    )(*args)


def exchange(blocks, axes):
    return lax.all_to_all(blocks, axes, split_axis=0, concat_axis=0, tiled=True)


def partner(value, axis, flip):
    size = lax.axis_size(axis)
    return lax.ppermute(value, axis, [(i, i ^ flip) for i in range(size)])


def summed(blocks):
    acc = blocks[0].astype(F32)
    for j in range(1, blocks.shape[0]):
        acc = acc + blocks[j].astype(F32)
    return acc


def sum_kernel(blocks, out):
    acc = summed(blocks).astype(out.dtype)
    for j in range(out.shape[0]):
        out[j] = acc


def sum_copies(blocks, count, dtype):
    (out,) = local(sum_kernel, [shape((count,) + blocks.shape[1:], dtype)], [blocks])
    return out


def total_kernel(blocks, out):
    out[...] = summed(blocks)


def query_kernel(w_query, latents_t, out):
    part = lax.dot_general(
        w_query[...], latents_t[...], (((0,), (0,)), ((), ())), preferred_element_type=F32
    )
    n, each, _ = out.shape
    for j in range(n):
        out[j] = part[j * each : (j + 1) * each]


def prepare_kernel(place, tokens, w_key, w_value, keys, keys_t, values, tokens_t, other_t, own_t):
    key = dot(tokens[...], w_key[...])
    keys[...] = key.astype(BF16)
    keys_t[...] = key.T.astype(BF16)
    values[...] = dot(tokens[...], w_value[...]).astype(BF16)
    for x in range(4):
        for w in range(4):
            at = (x * 4 + w) * 128
            slab = tokens[:, at : at + 128].T
            for y in range(4):
                tokens_t[x * 4 + y, w * 32 : (w + 1) * 32, :] = slab[y * 32 : (y + 1) * 32, :]
    z, c = place[2], place[3]
    hops, depth, cols = own_t.shape
    half = depth // 2
    for k in range(hops):
        for core, out in ((c, own_t), (1 - c, other_t)):
            rows = pl.ds(pl.multiple_of(((z ^ k) * 2 + core) * cols, cols), cols)
            out[k, :half, :] = w_key[rows, :].T
            out[k, half:, :] = w_value[rows, :].T


def expo_of(place, h, query_t, keys):
    rows, lats = keys.shape[0], query_t.shape[1]
    cols = slice(h * HEAD_DIM, (h + 1) * HEAD_DIM)
    pos_t = place[0] * rows + lax.broadcasted_iota(jnp.int32, (rows, lats), 0)
    pos_q = place[1] + lax.broadcasted_iota(jnp.int32, (rows, lats), 1)
    scores = dot(keys[:, cols], query_t[cols, :]) * SCALE
    return jnp.where(pos_t <= pos_q, jnp.exp(scores), 0.0)


def dprob_of(h, values, cot):
    cols = slice(h * HEAD_DIM, (h + 1) * HEAD_DIM)
    return dot_nt(values[:, cols], cot[:, cols])


def split(value):
    high = value.astype(BF16)
    return high, (value - high.astype(F32)).astype(BF16)


def dot_split(a, value):
    high, low = split(value)
    return dot(a, high) + dot(a, low)


def expo_kernel(place, query_t, keys, keys_t, values, cot, spread):
    heads = keys.shape[1] // HEAD_DIM
    n = spread.shape[0]
    each = keys.shape[1] // n
    per_head = n // heads
    sums = []
    for h in range(heads):
        cols = slice(h * HEAD_DIM, (h + 1) * HEAD_DIM)
        expo = expo_of(place, h, query_t, keys)
        weighted = expo * (dprob_of(h, values, cot) * SHRINK)
        sums.append(jnp.sum(expo, axis=0, keepdims=True))
        sums.append(jnp.sum(weighted, axis=0, keepdims=True))
        first = dot_split(keys_t[cols, :], weighted)
        second = dot_split(keys_t[cols, :], expo)
        for j in range(per_head):
            rows = slice(j * each, (j + 1) * each)
            spread[h * per_head + j, :each, :] = first[rows, :]
            spread[h * per_head + j, each : 2 * each, :] = second[rows, :]
    packed = jnp.concatenate(sums + sums, axis=0)
    for j in range(n):
        spread[j, 2 * each :, :] = packed


def grad_kernel(
    place, sums4, query_t, keys, values, cot, tokens_hbm, other_hbm, blocks, both, other, tokens_t, other_t, sems
):
    fetch = pltpu.make_async_copy(tokens_hbm, tokens_t, sems.at[0])
    fetch_other = pltpu.make_async_copy(other_hbm, other_t, sems.at[1])
    fetch.start()
    fetch_other.start()
    heads = keys.shape[1] // HEAD_DIM
    sums = summed(sums4)
    n, held, _ = blocks.shape
    depth = tokens_t.shape[1]
    each = held - depth
    denoms, deltas = [], []
    for h in range(heads):
        cols = slice(h * HEAD_DIM, (h + 1) * HEAD_DIM)
        at = 2 * each + 2 * h
        denom = sums[at : at + 1, :]
        shrunk = sums[at + 1 : at + 2, :] / denom
        delta = shrunk * (1.0 / SHRINK)
        denoms.append(denom)
        deltas.append(shrunk)
        probs = expo_of(place, h, query_t, keys) / denom
        grad = (probs * (dprob_of(h, values, cot) - delta) * SCALE).astype(BF16)
        both[:, cols] = dot_nt(grad, query_t[cols, :]).astype(BF16)
        value_cols = slice((heads + h) * HEAD_DIM, (heads + h + 1) * HEAD_DIM)
        both[:, value_cols] = dot(probs.astype(BF16), cot[:, cols]).astype(BF16)
    first_head = place[4] * heads < n
    denom = jnp.where(first_head, denoms[0], denoms[1])
    shrunk = jnp.where(first_head, deltas[0], deltas[1])
    query_grad = (sums[:each] - shrunk * sums[each : 2 * each]) / denom * (SCALE / SHRINK)
    query_grad = query_grad.astype(BF16)
    fetch.wait()
    tall = 4
    for j in range(0, n, tall):
        part = dot(tokens_t[j : j + tall].reshape(tall * depth, -1), both[...]).astype(BF16)
        for i in range(tall):
            blocks[j + i, :depth, :] = part[i * depth : (i + 1) * depth]
            blocks[j + i, depth:, :] = query_grad
    fetch_other.wait()
    for k in range(other.shape[0]):
        other[k] = dot(both[...], other_t[k]).astype(BF16)


def pair_kernel(both, weights, other, here, *away):
    here[...] = dot(both[...], weights[0]) + other[0].astype(F32)
    for k, out in enumerate(away):
        out[...] = (dot(both[...], weights[k + 1]) + other[k + 1].astype(F32)).astype(BF16)


def token_sum_kernel(here, one, two, three, out):
    total = here[...] + one[...].astype(F32) + two[...].astype(F32) + three[...].astype(F32)
    out[...] = total.astype(BF16)


def latent_sum_kernel(place, own, two, three, one, out, terms):
    for k, term in enumerate((own, one, two, three)):
        terms[k] = term[...].astype(F32)
    z = place[2]
    out[...] = ((terms[z] + terms[z ^ 1]) + terms[z ^ 2]) + terms[z ^ 3]


def near_sum_kernel(arrived, out):
    acc = summed(arrived)
    share = out.shape[1]
    for w in range(out.shape[0]):
        out[w] = acc[w * share : (w + 1) * share].astype(BF16)


def far_sum_kernel(arrived, key_weight, value_weight):
    width = key_weight.shape[1]
    acc = summed(arrived)
    key_weight[...] = acc[:, :width]
    value_weight[...] = acc[:, width:]


def on_device(tokens, latents, w_query, w_key, w_value, cotangent):
    rows, depth = tokens.shape
    lats = latents.shape[0]
    width = w_key.shape[1]
    heads = width // HEAD_DIM
    near, far = lax.axis_size(NEAR), lax.axis_size("w")
    n_seq = lax.axis_size(SEQ)
    n_head = lax.axis_size(HEAD)
    share = depth // n_seq
    each = width // near
    z, c = lax.axis_index("z"), lax.axis_index("c")
    place = jnp.stack([lax.axis_index(SEQ), rows * n_seq - lats, z, c, lax.axis_index(NEAR)])
    place = place.astype(jnp.int32)
    scalars = {0: SMEM}

    (query_part,) = local(
        query_kernel, [shape((near, each, lats), F32)], [w_query, latents.T], 2 * share * width * lats, limit=60
    )
    query_part = exchange(query_part, NEAR)
    block = depth // n_head
    hops = n_head // 2
    keys, keys_t, values, tokens_t, other_t, own_t = local(
        prepare_kernel,
        [
            shape((rows, width), BF16),
            shape((width, rows), BF16),
            shape((rows, width), BF16),
            shape((near, depth // near, rows), BF16),
            shape((hops, 2 * width, block), BF16),
            shape((hops, 2 * width, block), BF16),
        ],
        [place, tokens, w_key, w_value],
        2 * rows * depth * 2 * width,
        specs=scalars,
        limit=60,
    )

    query_part = exchange(sum_copies(query_part, far, F32), "w")
    query_part, keys, keys_t, values, tokens_t, other_t, own_t = lax.optimization_barrier(
        (query_part, keys, keys_t, values, tokens_t, other_t, own_t)
    )
    query_t = exchange(sum_copies(query_part, near, BF16), NEAR).reshape(width, lats)

    (spread,) = local(
        expo_kernel,
        [shape((near, 2 * each + 4 * heads, lats), F32)],
        [place, query_t, keys, keys_t, values, cotangent],
        12 * rows * width * lats,
        specs=scalars,
        limit=60,
    )
    sums = exchange(sum_copies(exchange(spread, NEAR), far, F32), "w")

    blocks, both, other = local(
        grad_kernel,
        [
            shape((near, depth // near + each, 2 * width), BF16),
            shape((rows, 2 * width), BF16),
            shape((hops, rows, block), BF16),
        ],
        [place, sums, query_t, keys, values, cotangent, tokens_t, other_t],
        8 * rows * width * lats + 3 * rows * depth * 2 * width,
        specs={0: SMEM, 6: HBM, 7: HBM},
        scratch=[
            pltpu.VMEM(tokens_t.shape, BF16),
            pltpu.VMEM(other_t.shape, BF16),
            pltpu.SemaphoreType.DMA((2,)),
        ],
        limit=60,
    )
    arrived = exchange(blocks, NEAR)

    here, *away = local(
        pair_kernel,
        [shape((rows, block), F32)] + [shape((rows, block), BF16)] * (hops - 1),
        [both, own_t, partner(other, "c", 1)],
        rows * depth * 2 * width,
        limit=60,
    )
    parts = [partner(away[k - 1], "z", k) for k in (2, 3, 1)]
    (token_grad,) = local(token_sum_kernel, [shape((rows, block), BF16)], [here, *parts], limit=60)
    arrived, token_grad = lax.optimization_barrier((arrived, token_grad))

    (sent,) = local(
        near_sum_kernel,
        [shape((far, share, 2 * width), BF16)],
        [arrived],
        specs={0: pl.BlockSpec((near, depth // near, 2 * width), lambda i: (0, 0, 0))},
    )
    query_grad_t = arrived[:, depth // near :, :].reshape(width, lats)
    sent, query_grad_t = lax.optimization_barrier((sent, query_grad_t))
    key_weight_grad, value_weight_grad = local(
        far_sum_kernel, [shape((share, width), F32)] * 2, [exchange(sent, "w")]
    )
    latent_grad_t = dot(w_query, query_grad_t)
    query_weight_grad = lax.dot_general(
        latents, query_grad_t, (((0,), (1,)), ((), ())), preferred_element_type=F32
    )
    held = latent_grad_t.astype(BF16)
    held = (held.astype(F32) + partner(held, "c", 1).astype(F32)).astype(BF16)
    (latent_grad_t,) = local(
        latent_sum_kernel,
        [shape((share, lats), F32)],
        [place, held] + [partner(held, "z", k) for k in (2, 3, 1)],
        specs=scalars,
        scratch=[pltpu.VMEM((hops, share, lats), F32)],
    )
    return (
        token_grad,
        latent_grad_t.T,
        query_weight_grad,
        key_weight_grad,
        value_weight_grad,
    )


def solution(mesh):
    fine = Mesh(mesh.devices.reshape(4, 4, 4, 4, 2), ("x", "w", "y", "z", "c"))
    placed = (
        P(SEQ, None),
        P(None, SEQ),
        P(SEQ, HEAD),
        P(None, HEAD),
        P(None, HEAD),
        P(None, HEAD),
    )
    return jax.shard_map(
        on_device,
        mesh=fine,
        in_specs=placed,
        out_specs=(
            P(SEQ, HEAD),
            P(None, SEQ),
            P(SEQ, HEAD),
            P(SEQ, HEAD),
            P(SEQ, HEAD),
        ),
        check_vma=False,
    )
```

```python
import jax
import jax.numpy as jnp
from jax import lax
from jax.experimental import pallas as pl
from jax.experimental.pallas import tpu as pltpu
from jax.sharding import Mesh
from jax.sharding import PartitionSpec as P

HEAD_DIM = 128
SCALE = HEAD_DIM ** (-0.5)
SEQ = ("x", "w", "y")
HEAD = ("z", "c")
NEAR = ("x", "y")
F32 = jnp.float32
BF16 = jnp.bfloat16
SMEM = pl.BlockSpec(memory_space=pltpu.SMEM)
HBM = pl.BlockSpec(memory_space=pl.ANY)
NT = (((1,), (1,)), ((), ()))
MIB = 1024 * 1024
SHRINK = 2.0**-12


def dot(a, b):
    return jnp.dot(a, b, preferred_element_type=F32)


def dot_nt(a, b):
    return lax.dot_general(a, b, NT, preferred_element_type=F32)


def shape(dims, dtype):
    return jax.ShapeDtypeStruct(dims, dtype)


def whole(array):
    rank = len(array.shape)
    return pl.BlockSpec(array.shape, lambda i: (0,) * rank)


def local(body, outs, args, flops=0, specs=None, grid=1, out_specs=None, scratch=(), limit=16):
    specs = specs or {}
    moved = sum(a.size * a.dtype.itemsize for a in list(args) + list(outs))
    return pl.pallas_call(
        body,
        out_shape=outs,
        grid=(grid,),
        in_specs=[specs.get(i) or whole(a) for i, a in enumerate(args)],
        out_specs=out_specs or [whole(o) for o in outs],
        scratch_shapes=list(scratch),
        compiler_params=pltpu.CompilerParams(vmem_limit_bytes=limit * MIB),
        cost_estimate=pl.CostEstimate(flops=flops, bytes_accessed=moved, transcendentals=0),
    )(*args)


def exchange(blocks, axes):
    return lax.all_to_all(blocks, axes, split_axis=0, concat_axis=0, tiled=True)


def partner(value, axis, flip):
    size = lax.axis_size(axis)
    return lax.ppermute(value, axis, [(i, i ^ flip) for i in range(size)])


def summed(blocks):
    acc = blocks[0].astype(F32)
    for j in range(1, blocks.shape[0]):
        acc = acc + blocks[j].astype(F32)
    return acc


def sum_kernel(blocks, out):
    acc = summed(blocks).astype(out.dtype)
    for j in range(out.shape[0]):
        out[j] = acc


def sum_copies(blocks, count, dtype):
    (out,) = local(sum_kernel, [shape((count,) + blocks.shape[1:], dtype)], [blocks])
    return out


def total_kernel(blocks, out):
    out[...] = summed(blocks)


def query_kernel(w_query, latents_t, out):
    part = lax.dot_general(
        w_query[...], latents_t[...], (((0,), (0,)), ((), ())), preferred_element_type=F32
    )
    n, each, _ = out.shape
    for j in range(n):
        out[j] = part[j * each : (j + 1) * each]


def prepare_kernel(place, tokens, w_key, w_value, keys, keys_t, values, tokens_t, other_t, own_t):
    key = dot(tokens[...], w_key[...])
    keys[...] = key.astype(BF16)
    keys_t[...] = key.T.astype(BF16)
    values[...] = dot(tokens[...], w_value[...]).astype(BF16)
    for x in range(4):
        for w in range(4):
            at = (x * 4 + w) * 128
            slab = tokens[:, at : at + 128].T
            for y in range(4):
                tokens_t[x * 4 + y, w * 32 : (w + 1) * 32, :] = slab[y * 32 : (y + 1) * 32, :]
    z, c = place[2], place[3]
    hops, depth, cols = own_t.shape
    half = depth // 2
    for k in range(hops):
        for core, out in ((c, own_t), (1 - c, other_t)):
            rows = pl.ds(pl.multiple_of(((z ^ k) * 2 + core) * cols, cols), cols)
            out[k, :half, :] = w_key[rows, :].T
            out[k, half:, :] = w_value[rows, :].T


def expo_of(place, h, query_t, keys):
    rows, lats = keys.shape[0], query_t.shape[1]
    cols = slice(h * HEAD_DIM, (h + 1) * HEAD_DIM)
    pos_t = place[0] * rows + lax.broadcasted_iota(jnp.int32, (rows, lats), 0)
    pos_q = place[1] + lax.broadcasted_iota(jnp.int32, (rows, lats), 1)
    scores = dot(keys[:, cols], query_t[cols, :]) * SCALE
    return jnp.where(pos_t <= pos_q, jnp.exp(scores), 0.0)


def dprob_of(h, values, cot):
    cols = slice(h * HEAD_DIM, (h + 1) * HEAD_DIM)
    return dot_nt(values[:, cols], cot[:, cols])


def split(value):
    high = value.astype(BF16)
    return high, (value - high.astype(F32)).astype(BF16)


def dot_split(a, value):
    high, low = split(value)
    return dot(a, high) + dot(a, low)


def pack_sums(sums):
    high = sums.astype(BF16).astype(F32)
    middle = (sums - high).astype(BF16).astype(F32)
    low = sums - high - middle
    return jnp.concatenate([high, middle, low, jnp.zeros_like(sums)], axis=0).astype(BF16)


def unpack_sums(rows):
    rows = rows.astype(F32)
    return rows[0:4] + rows[4:8] + rows[8:12]


def mean_of(numer, denom):
    return jnp.where(denom > 0, numer / jnp.where(denom > 0, denom, 1.0), 0.0)


def mine_of(sums, place):
    first = place[4] < 8
    return jnp.where(first, sums[0:1], sums[2:3]), jnp.where(first, sums[1:2], sums[3:4])


def expo_kernel(place, query_t, keys, keys_t, values, cot, spread):
    heads = keys.shape[1] // HEAD_DIM
    n = spread.shape[0]
    each = keys.shape[1] // n
    per_head = n // heads
    sums = []
    for h in range(heads):
        cols = slice(h * HEAD_DIM, (h + 1) * HEAD_DIM)
        expo = expo_of(place, h, query_t, keys)
        weighted = expo * (dprob_of(h, values, cot) * SHRINK)
        denom = jnp.sum(expo, axis=0, keepdims=True)
        numer = jnp.sum(weighted, axis=0, keepdims=True)
        sums += [denom, numer]
        second = dot_split(keys_t[cols, :], expo)
        first = dot_split(keys_t[cols, :], weighted) - mean_of(numer, denom) * second
        first, second = first.astype(BF16), second.astype(BF16)
        for j in range(per_head):
            rows = slice(j * each, (j + 1) * each)
            spread[h * per_head + j, :each, :] = first[rows, :]
            spread[h * per_head + j, each : 2 * each, :] = second[rows, :]
    packed = pack_sums(jnp.concatenate(sums, axis=0))
    for j in range(n):
        spread[j, 2 * each :, :] = packed


def gathered(blocks, place):
    each = (blocks.shape[1] - 16) // 2
    sent = [unpack_sums(blocks[d, 2 * each :, :]) for d in range(blocks.shape[0])]
    sums = sent[0]
    for part in sent[1:]:
        sums = sums + part
    denom, numer = mine_of(sums, place)
    mean = mean_of(numer, denom)
    first = second = 0.0
    for d, part in enumerate(sent):
        denom_d, numer_d = mine_of(part, place)
        rows = blocks[d, each : 2 * each, :].astype(F32)
        first = first + blocks[d, :each, :].astype(F32) + (mean_of(numer_d, denom_d) - mean) * rows
        second = second + rows
    return sums, first, second


def sums_kernel(place, blocks, out):
    sums, first, second = gathered(blocks, place)
    each = first.shape[0]
    first, second, packed = first.astype(BF16), second.astype(BF16), pack_sums(sums)
    for j in range(out.shape[0]):
        out[j, :each, :] = first
        out[j, each : 2 * each, :] = second
        out[j, 2 * each :, :] = packed


def grad_kernel(
    place, sums4, query_t, keys, values, cot, tokens_hbm, other_hbm, blocks, both, other, tokens_t, other_t, sems
):
    fetch = pltpu.make_async_copy(tokens_hbm, tokens_t, sems.at[0])
    fetch_other = pltpu.make_async_copy(other_hbm, other_t, sems.at[1])
    fetch.start()
    fetch_other.start()
    heads = keys.shape[1] // HEAD_DIM
    sums, centred, _ = gathered(sums4, place)
    n, held, _ = blocks.shape
    depth = tokens_t.shape[1]
    each = held - depth
    for h in range(heads):
        cols = slice(h * HEAD_DIM, (h + 1) * HEAD_DIM)
        denom = sums[2 * h : 2 * h + 1, :]
        delta = sums[2 * h + 1 : 2 * h + 2, :] / denom * (1.0 / SHRINK)
        probs = expo_of(place, h, query_t, keys) / denom
        grad = (probs * (dprob_of(h, values, cot) - delta) * SCALE).astype(BF16)
        both[:, cols] = dot_nt(grad, query_t[cols, :]).astype(BF16)
        value_cols = slice((heads + h) * HEAD_DIM, (heads + h + 1) * HEAD_DIM)
        both[:, value_cols] = dot(probs.astype(BF16), cot[:, cols]).astype(BF16)
    query_grad = (centred / mine_of(sums, place)[0] * (SCALE / SHRINK)).astype(BF16)
    fetch.wait()
    tall = 4
    for j in range(0, n, tall):
        part = dot(tokens_t[j : j + tall].reshape(tall * depth, -1), both[...]).astype(BF16)
        for i in range(tall):
            blocks[j + i, :depth, :] = part[i * depth : (i + 1) * depth]
            blocks[j + i, depth:, :] = query_grad
    fetch_other.wait()
    for k in range(other.shape[0]):
        other[k] = dot(both[...], other_t[k]).astype(BF16)


def pair_kernel(both, weights, other, here, *away):
    here[...] = dot(both[...], weights[0]) + other[0].astype(F32)
    for k, out in enumerate(away):
        out[...] = (dot(both[...], weights[k + 1]) + other[k + 1].astype(F32)).astype(BF16)


def token_sum_kernel(here, one, two, three, out):
    total = here[...] + one[...].astype(F32) + two[...].astype(F32) + three[...].astype(F32)
    out[...] = total.astype(BF16)


def latent_sum_kernel(place, own, two, three, one, out, terms):
    for k, term in enumerate((own, one, two, three)):
        terms[k] = term[...].astype(F32)
    z = place[2]
    out[...] = ((terms[z] + terms[z ^ 1]) + terms[z ^ 2]) + terms[z ^ 3]


def near_sum_kernel(arrived, out):
    acc = summed(arrived)
    share = out.shape[1]
    for w in range(out.shape[0]):
        out[w] = acc[w * share : (w + 1) * share].astype(BF16)


def far_sum_kernel(arrived, key_weight, value_weight):
    width = key_weight.shape[1]
    acc = summed(arrived)
    key_weight[...] = acc[:, :width]
    value_weight[...] = acc[:, width:]


def on_device(tokens, latents, w_query, w_key, w_value, cotangent):
    rows, depth = tokens.shape
    lats = latents.shape[0]
    width = w_key.shape[1]
    heads = width // HEAD_DIM
    near, far = lax.axis_size(NEAR), lax.axis_size("w")
    n_seq = lax.axis_size(SEQ)
    n_head = lax.axis_size(HEAD)
    share = depth // n_seq
    each = width // near
    z, c = lax.axis_index("z"), lax.axis_index("c")
    place = jnp.stack([lax.axis_index(SEQ), rows * n_seq - lats, z, c, lax.axis_index(NEAR)])
    place = place.astype(jnp.int32)
    scalars = {0: SMEM}

    (query_part,) = local(
        query_kernel, [shape((near, each, lats), F32)], [w_query, latents.T], 2 * share * width * lats, limit=60
    )
    query_part = exchange(query_part, NEAR)
    block = depth // n_head
    hops = n_head // 2
    keys, keys_t, values, tokens_t, other_t, own_t = local(
        prepare_kernel,
        [
            shape((rows, width), BF16),
            shape((width, rows), BF16),
            shape((rows, width), BF16),
            shape((near, depth // near, rows), BF16),
            shape((hops, 2 * width, block), BF16),
            shape((hops, 2 * width, block), BF16),
        ],
        [place, tokens, w_key, w_value],
        2 * rows * depth * 2 * width,
        specs=scalars,
        limit=60,
    )

    query_part = exchange(sum_copies(query_part, far, F32), "w")
    query_part, keys, keys_t, values, tokens_t, other_t, own_t = lax.optimization_barrier(
        (query_part, keys, keys_t, values, tokens_t, other_t, own_t)
    )
    query_t = exchange(sum_copies(query_part, near, BF16), NEAR).reshape(width, lats)

    (spread,) = local(
        expo_kernel,
        [shape((near, 2 * each + 16, lats), BF16)],
        [place, query_t, keys, keys_t, values, cotangent],
        12 * rows * width * lats,
        specs=scalars,
        limit=60,
    )
    (spread,) = local(
        sums_kernel,
        [shape((far,) + spread.shape[1:], BF16)],
        [place, exchange(spread, NEAR)],
        specs=scalars,
    )
    sums = exchange(spread, "w")

    blocks, both, other = local(
        grad_kernel,
        [
            shape((near, depth // near + each, 2 * width), BF16),
            shape((rows, 2 * width), BF16),
            shape((hops, rows, block), BF16),
        ],
        [place, sums, query_t, keys, values, cotangent, tokens_t, other_t],
        8 * rows * width * lats + 3 * rows * depth * 2 * width,
        specs={0: SMEM, 6: HBM, 7: HBM},
        scratch=[
            pltpu.VMEM(tokens_t.shape, BF16),
            pltpu.VMEM(other_t.shape, BF16),
            pltpu.SemaphoreType.DMA((2,)),
        ],
        limit=60,
    )
    arrived = exchange(blocks, NEAR)

    here, *away = local(
        pair_kernel,
        [shape((rows, block), F32)] + [shape((rows, block), BF16)] * (hops - 1),
        [both, own_t, partner(other, "c", 1)],
        rows * depth * 2 * width,
        limit=60,
    )
    parts = [partner(away[k - 1], "z", k) for k in (2, 3, 1)]
    (token_grad,) = local(token_sum_kernel, [shape((rows, block), BF16)], [here, *parts], limit=60)
    arrived, token_grad = lax.optimization_barrier((arrived, token_grad))

    (sent,) = local(
        near_sum_kernel,
        [shape((far, share, 2 * width), BF16)],
        [arrived],
        specs={0: pl.BlockSpec((near, depth // near, 2 * width), lambda i: (0, 0, 0))},
    )
    query_grad_t = arrived[:, depth // near :, :].reshape(width, lats)
    sent, query_grad_t = lax.optimization_barrier((sent, query_grad_t))
    key_weight_grad, value_weight_grad = local(
        far_sum_kernel, [shape((share, width), F32)] * 2, [exchange(sent, "w")]
    )
    latent_grad_t = dot(w_query, query_grad_t)
    query_weight_grad = lax.dot_general(
        latents, query_grad_t, (((0,), (1,)), ((), ())), preferred_element_type=F32
    )
    held = latent_grad_t.astype(BF16)
    held = (held.astype(F32) + partner(held, "c", 1).astype(F32)).astype(BF16)
    (latent_grad_t,) = local(
        latent_sum_kernel,
        [shape((share, lats), F32)],
        [place, held] + [partner(held, "z", k) for k in (2, 3, 1)],
        specs=scalars,
        scratch=[pltpu.VMEM((hops, share, lats), F32)],
    )
    return (
        token_grad,
        latent_grad_t.T,
        query_weight_grad,
        key_weight_grad,
        value_weight_grad,
    )


def solution(mesh):
    fine = Mesh(mesh.devices.reshape(4, 4, 4, 4, 2), ("x", "w", "y", "z", "c"))
    placed = (
        P(SEQ, None),
        P(None, SEQ),
        P(SEQ, HEAD),
        P(None, HEAD),
        P(None, HEAD),
        P(None, HEAD),
    )
    return jax.shard_map(
        on_device,
        mesh=fine,
        in_specs=placed,
        out_specs=(
            P(SEQ, HEAD),
            P(None, SEQ),
            P(SEQ, HEAD),
            P(SEQ, HEAD),
            P(SEQ, HEAD),
        ),
        check_vma=False,
    )
```

```python
import jax
import jax.numpy as jnp
from jax import lax
from jax.experimental import pallas as pl
from jax.experimental.pallas import tpu as pltpu
from jax.sharding import Mesh
from jax.sharding import PartitionSpec as P

HEAD_DIM = 128
SCALE = HEAD_DIM ** (-0.5)
SEQ = ("x", "w", "y")
HEAD = ("z", "c")
NEAR = ("x", "y")
F32 = jnp.float32
BF16 = jnp.bfloat16
SMEM = pl.BlockSpec(memory_space=pltpu.SMEM)
HBM = pl.BlockSpec(memory_space=pl.ANY)
NT = (((1,), (1,)), ((), ()))
MIB = 1024 * 1024
SHRINK = 2.0**-12


def dot(a, b):
    return jnp.dot(a, b, preferred_element_type=F32)


def dot_nt(a, b):
    return lax.dot_general(a, b, NT, preferred_element_type=F32)


def shape(dims, dtype):
    return jax.ShapeDtypeStruct(dims, dtype)


def whole(array):
    rank = len(array.shape)
    return pl.BlockSpec(array.shape, lambda i: (0,) * rank)


def local(body, outs, args, flops=0, specs=None, grid=1, out_specs=None, scratch=(), limit=16):
    specs = specs or {}
    moved = sum(a.size * a.dtype.itemsize for a in list(args) + list(outs))
    return pl.pallas_call(
        body,
        out_shape=outs,
        grid=(grid,),
        in_specs=[specs.get(i) or whole(a) for i, a in enumerate(args)],
        out_specs=out_specs or [whole(o) for o in outs],
        scratch_shapes=list(scratch),
        compiler_params=pltpu.CompilerParams(vmem_limit_bytes=limit * MIB),
        cost_estimate=pl.CostEstimate(flops=flops, bytes_accessed=moved, transcendentals=0),
    )(*args)


def exchange(blocks, axes):
    return lax.all_to_all(blocks, axes, split_axis=0, concat_axis=0, tiled=True)


def partner(value, axis, flip):
    size = lax.axis_size(axis)
    return lax.ppermute(value, axis, [(i, i ^ flip) for i in range(size)])


def summed(blocks):
    acc = blocks[0].astype(F32)
    for j in range(1, blocks.shape[0]):
        acc = acc + blocks[j].astype(F32)
    return acc


def sum_kernel(blocks, out):
    acc = summed(blocks).astype(out.dtype)
    for j in range(out.shape[0]):
        out[j] = acc


def sum_copies(blocks, count, dtype):
    (out,) = local(sum_kernel, [shape((count,) + blocks.shape[1:], dtype)], [blocks])
    return out


def total_kernel(blocks, out):
    out[...] = summed(blocks)


def query_kernel(w_query, latents_t, out):
    part = lax.dot_general(
        w_query[...], latents_t[...], (((0,), (0,)), ((), ())), preferred_element_type=F32
    )
    n, each, _ = out.shape
    for j in range(n):
        out[j] = part[j * each : (j + 1) * each]


def prepare_kernel(place, tokens, w_key, w_value, keys, keys_t, values, tokens_t, other_t, own_t):
    key = dot(tokens[...], w_key[...])
    keys[...] = key.astype(BF16)
    keys_t[...] = key.T.astype(BF16)
    values[...] = dot(tokens[...], w_value[...]).astype(BF16)
    for x in range(4):
        for w in range(4):
            at = (x * 4 + w) * 128
            slab = tokens[:, at : at + 128].T
            for y in range(4):
                tokens_t[x * 4 + y, w * 32 : (w + 1) * 32, :] = slab[y * 32 : (y + 1) * 32, :]
    z, c = place[2], place[3]
    hops, depth, cols = own_t.shape
    half = depth // 2
    for k in range(hops):
        for core, out in ((c, own_t), (1 - c, other_t)):
            rows = pl.ds(pl.multiple_of(((z ^ k) * 2 + core) * cols, cols), cols)
            out[k, :half, :] = w_key[rows, :].T
            out[k, half:, :] = w_value[rows, :].T


def expo_of(place, h, query_t, keys):
    rows, lats = keys.shape[0], query_t.shape[1]
    cols = slice(h * HEAD_DIM, (h + 1) * HEAD_DIM)
    pos_t = place[0] * rows + lax.broadcasted_iota(jnp.int32, (rows, lats), 0)
    pos_q = place[1] + lax.broadcasted_iota(jnp.int32, (rows, lats), 1)
    scores = dot(keys[:, cols], query_t[cols, :]) * SCALE
    return jnp.where(pos_t <= pos_q, jnp.exp(scores), 0.0)


def dprob_of(h, values, cot):
    cols = slice(h * HEAD_DIM, (h + 1) * HEAD_DIM)
    return dot_nt(values[:, cols], cot[:, cols])


def split(value):
    high = value.astype(BF16)
    return high, (value - high.astype(F32)).astype(BF16)


def dot_split(a, value):
    high, low = split(value)
    return dot(a, high) + dot(a, low)


def pack_sums(sums):
    high = sums.astype(BF16).astype(F32)
    middle = (sums - high).astype(BF16).astype(F32)
    low = sums - high - middle
    return jnp.concatenate([high, middle, low, jnp.zeros_like(sums)], axis=0).astype(BF16)


def unpack_sums(rows):
    rows = rows.astype(F32)
    return rows[0:4] + rows[4:8] + rows[8:12]


def mean_of(numer, denom):
    return jnp.where(denom > 0, numer / jnp.where(denom > 0, denom, 1.0), 0.0)


def mine_of(sums, place):
    first = place[4] < 8
    return jnp.where(first, sums[0:1], sums[2:3]), jnp.where(first, sums[1:2], sums[3:4])


def expo_kernel(place, query_t, keys, keys_t, values, cot, spread):
    heads = keys.shape[1] // HEAD_DIM
    n = spread.shape[0]
    each = keys.shape[1] // n
    per_head = n // heads
    sums = []
    for h in range(heads):
        cols = slice(h * HEAD_DIM, (h + 1) * HEAD_DIM)
        expo = expo_of(place, h, query_t, keys)
        weighted = expo * (dprob_of(h, values, cot) * SHRINK)
        denom = jnp.sum(expo, axis=0, keepdims=True)
        numer = jnp.sum(weighted, axis=0, keepdims=True)
        sums += [denom, numer]
        second = dot_split(keys_t[cols, :], expo)
        first = dot_split(keys_t[cols, :], weighted) - mean_of(numer, denom) * second
        first, second = first.astype(BF16), second.astype(BF16)
        for j in range(per_head):
            rows = slice(j * each, (j + 1) * each)
            spread[h * per_head + j, :each, :] = first[rows, :]
            spread[h * per_head + j, each : 2 * each, :] = second[rows, :]
    packed = pack_sums(jnp.concatenate(sums, axis=0))
    for j in range(n):
        spread[j, 2 * each :, :] = packed


def gathered(blocks, place):
    each = (blocks.shape[1] - 16) // 2
    sent = [unpack_sums(blocks[d, 2 * each :, :]) for d in range(blocks.shape[0])]
    sums = sent[0]
    for part in sent[1:]:
        sums = sums + part
    denom, numer = mine_of(sums, place)
    mean = mean_of(numer, denom)
    first = second = 0.0
    for d, part in enumerate(sent):
        denom_d, numer_d = mine_of(part, place)
        rows = blocks[d, each : 2 * each, :].astype(F32)
        first = first + blocks[d, :each, :].astype(F32) + (mean_of(numer_d, denom_d) - mean) * rows
        second = second + rows
    return sums, first, second


def sums_kernel(place, blocks, out):
    sums, first, second = gathered(blocks, place)
    each = first.shape[0]
    first, second, packed = first.astype(BF16), second.astype(BF16), pack_sums(sums)
    for j in range(out.shape[0]):
        out[j, :each, :] = first
        out[j, each : 2 * each, :] = second
        out[j, 2 * each :, :] = packed


def grad_kernel(
    place, sums4, query_t, keys, values, cot, tokens_hbm, other_hbm, blocks, both, other, tokens_t, other_t, sems
):
    fetch = pltpu.make_async_copy(tokens_hbm, tokens_t, sems.at[0])
    fetch_other = pltpu.make_async_copy(other_hbm, other_t, sems.at[1])
    fetch.start()
    fetch_other.start()
    heads = keys.shape[1] // HEAD_DIM
    sums, centred, _ = gathered(sums4, place)
    n, held, _ = blocks.shape
    depth = tokens_t.shape[1]
    each = held - depth
    for h in range(heads):
        cols = slice(h * HEAD_DIM, (h + 1) * HEAD_DIM)
        denom = sums[2 * h : 2 * h + 1, :]
        delta = sums[2 * h + 1 : 2 * h + 2, :] / denom * (1.0 / SHRINK)
        probs = expo_of(place, h, query_t, keys) / denom
        grad = (probs * (dprob_of(h, values, cot) - delta) * SCALE).astype(BF16)
        both[:, cols] = dot_nt(grad, query_t[cols, :]).astype(BF16)
        value_cols = slice((heads + h) * HEAD_DIM, (heads + h + 1) * HEAD_DIM)
        both[:, value_cols] = dot(probs.astype(BF16), cot[:, cols]).astype(BF16)
    query_grad = (centred / mine_of(sums, place)[0] * (SCALE / SHRINK)).astype(BF16)
    fetch.wait()
    tall = 4
    for j in range(0, n, tall):
        part = dot(tokens_t[j : j + tall].reshape(tall * depth, -1), both[...]).astype(BF16)
        for i in range(tall):
            blocks[j + i, :depth, :] = part[i * depth : (i + 1) * depth]
            blocks[j + i, depth:, :] = query_grad
    fetch_other.wait()
    for k in range(other.shape[0]):
        other[k] = dot(both[...], other_t[k]).astype(BF16)


def pair_kernel(both, weights, other, here, *away):
    here[...] = dot(both[...], weights[0]) + other[0].astype(F32)
    for k, out in enumerate(away):
        out[...] = (dot(both[...], weights[k + 1]) + other[k + 1].astype(F32)).astype(BF16)


def token_sum_kernel(here, one, two, three, out):
    total = here[...] + one[...].astype(F32) + two[...].astype(F32) + three[...].astype(F32)
    out[...] = total.astype(BF16)


def latent_sum_kernel(place, own, two, three, one, out, terms):
    for k, term in enumerate((own, one, two, three)):
        terms[k] = term[...].astype(F32)
    z = place[2]
    out[...] = ((terms[z] + terms[z ^ 1]) + terms[z ^ 2]) + terms[z ^ 3]


def near_sum_kernel(arrived, out):
    acc = summed(arrived)
    share = out.shape[1]
    for w in range(out.shape[0]):
        out[w] = acc[w * share : (w + 1) * share].astype(BF16)


def far_sum_kernel(arrived, key_weight, value_weight):
    width = key_weight.shape[1]
    acc = summed(arrived)
    key_weight[...] = acc[:, :width]
    value_weight[...] = acc[:, width:]


def on_device(tokens, latents, w_query, w_key, w_value, cotangent):
    rows, depth = tokens.shape
    lats = latents.shape[0]
    width = w_key.shape[1]
    heads = width // HEAD_DIM
    near, far = lax.axis_size(NEAR), lax.axis_size("w")
    n_seq = lax.axis_size(SEQ)
    n_head = lax.axis_size(HEAD)
    share = depth // n_seq
    each = width // near
    z, c = lax.axis_index("z"), lax.axis_index("c")
    place = jnp.stack([lax.axis_index(SEQ), rows * n_seq - lats, z, c, lax.axis_index(NEAR)])
    place = place.astype(jnp.int32)
    scalars = {0: SMEM}

    (query_part,) = local(
        query_kernel, [shape((near, each, lats), F32)], [w_query, latents.T], 2 * share * width * lats, limit=60
    )
    query_part = exchange(query_part, NEAR)
    block = depth // n_head
    hops = n_head // 2
    keys, keys_t, values, tokens_t, other_t, own_t = local(
        prepare_kernel,
        [
            shape((rows, width), BF16),
            shape((width, rows), BF16),
            shape((rows, width), BF16),
            shape((near, depth // near, rows), BF16),
            shape((hops, 2 * width, block), BF16),
            shape((hops, 2 * width, block), BF16),
        ],
        [place, tokens, w_key, w_value],
        2 * rows * depth * 2 * width,
        specs=scalars,
        limit=60,
    )

    query_part = exchange(sum_copies(query_part, far, BF16), "w")
    query_part, keys, keys_t, values, tokens_t, other_t, own_t = lax.optimization_barrier(
        (query_part, keys, keys_t, values, tokens_t, other_t, own_t)
    )
    query_t = exchange(sum_copies(query_part, near, BF16), NEAR).reshape(width, lats)

    (spread,) = local(
        expo_kernel,
        [shape((near, 2 * each + 16, lats), BF16)],
        [place, query_t, keys, keys_t, values, cotangent],
        12 * rows * width * lats,
        specs=scalars,
        limit=60,
    )
    (spread,) = local(
        sums_kernel,
        [shape((far,) + spread.shape[1:], BF16)],
        [place, exchange(spread, NEAR)],
        specs=scalars,
    )
    sums = exchange(spread, "w")

    blocks, both, other = local(
        grad_kernel,
        [
            shape((near, depth // near + each, 2 * width), BF16),
            shape((rows, 2 * width), BF16),
            shape((hops, rows, block), BF16),
        ],
        [place, sums, query_t, keys, values, cotangent, tokens_t, other_t],
        8 * rows * width * lats + 3 * rows * depth * 2 * width,
        specs={0: SMEM, 6: HBM, 7: HBM},
        scratch=[
            pltpu.VMEM(tokens_t.shape, BF16),
            pltpu.VMEM(other_t.shape, BF16),
            pltpu.SemaphoreType.DMA((2,)),
        ],
        limit=60,
    )
    arrived = exchange(blocks, NEAR)

    here, *away = local(
        pair_kernel,
        [shape((rows, block), F32)] + [shape((rows, block), BF16)] * (hops - 1),
        [both, own_t, partner(other, "c", 1)],
        rows * depth * 2 * width,
        limit=60,
    )
    parts = [partner(away[k - 1], "z", k) for k in (2, 3, 1)]
    arrived, here, *parts = lax.optimization_barrier((arrived, here, *parts))
    (token_grad,) = local(token_sum_kernel, [shape((rows, block), BF16)], [here, *parts], limit=60)

    (sent,) = local(
        near_sum_kernel,
        [shape((far, share, 2 * width), BF16)],
        [arrived],
        specs={0: pl.BlockSpec((near, depth // near, 2 * width), lambda i: (0, 0, 0))},
    )
    query_grad_t = arrived[:, depth // near :, :].reshape(width, lats)
    sent, query_grad_t = lax.optimization_barrier((sent, query_grad_t))
    key_weight_grad, value_weight_grad = local(
        far_sum_kernel, [shape((share, width), F32)] * 2, [exchange(sent, "w")]
    )
    latent_grad_t = dot(w_query, query_grad_t)
    query_weight_grad = lax.dot_general(
        latents, query_grad_t, (((0,), (1,)), ((), ())), preferred_element_type=F32
    )
    held = latent_grad_t.astype(BF16)
    held = (held.astype(F32) + partner(held, "c", 1).astype(F32)).astype(BF16)
    (latent_grad_t,) = local(
        latent_sum_kernel,
        [shape((share, lats), F32)],
        [place, held] + [partner(held, "z", k) for k in (2, 3, 1)],
        specs=scalars,
        scratch=[pltpu.VMEM((hops, share, lats), F32)],
    )
    return (
        token_grad,
        latent_grad_t.T,
        query_weight_grad,
        key_weight_grad,
        value_weight_grad,
    )


def solution(mesh):
    fine = Mesh(mesh.devices.reshape(4, 4, 4, 4, 2), ("x", "w", "y", "z", "c"))
    placed = (
        P(SEQ, None),
        P(None, SEQ),
        P(SEQ, HEAD),
        P(None, HEAD),
        P(None, HEAD),
        P(None, HEAD),
    )
    return jax.shard_map(
        on_device,
        mesh=fine,
        in_specs=placed,
        out_specs=(
            P(SEQ, HEAD),
            P(None, SEQ),
            P(SEQ, HEAD),
            P(SEQ, HEAD),
            P(SEQ, HEAD),
        ),
        check_vma=False,
    )
```

```python
import jax
import jax.numpy as jnp
from jax import lax
from jax.experimental import pallas as pl
from jax.experimental.pallas import tpu as pltpu
from jax.sharding import Mesh
from jax.sharding import PartitionSpec as P

HEAD_DIM = 128
SCALE = HEAD_DIM ** (-0.5)
SEQ = ("x", "w", "y")
HEAD = ("z", "c")
NEAR = ("x", "y")
F32 = jnp.float32
BF16 = jnp.bfloat16
SMEM = pl.BlockSpec(memory_space=pltpu.SMEM)
HBM = pl.BlockSpec(memory_space=pl.ANY)
NT = (((1,), (1,)), ((), ()))
MIB = 1024 * 1024
SHRINK = 2.0**-12


def dot(a, b):
    return jnp.dot(a, b, preferred_element_type=F32)


def dot_nt(a, b):
    return lax.dot_general(a, b, NT, preferred_element_type=F32)


def shape(dims, dtype):
    return jax.ShapeDtypeStruct(dims, dtype)


def whole(array):
    rank = len(array.shape)
    return pl.BlockSpec(array.shape, lambda i: (0,) * rank)


def local(body, outs, args, flops=0, specs=None, grid=1, out_specs=None, scratch=(), limit=16):
    specs = specs or {}
    moved = sum(a.size * a.dtype.itemsize for a in list(args) + list(outs))
    return pl.pallas_call(
        body,
        out_shape=outs,
        grid=(grid,),
        in_specs=[specs.get(i) or whole(a) for i, a in enumerate(args)],
        out_specs=out_specs or [whole(o) for o in outs],
        scratch_shapes=list(scratch),
        compiler_params=pltpu.CompilerParams(vmem_limit_bytes=limit * MIB),
        cost_estimate=pl.CostEstimate(flops=flops, bytes_accessed=moved, transcendentals=0),
    )(*args)


def exchange(blocks, axes):
    return lax.all_to_all(blocks, axes, split_axis=0, concat_axis=0, tiled=True)


def partner(value, axis, flip):
    size = lax.axis_size(axis)
    return lax.ppermute(value, axis, [(i, i ^ flip) for i in range(size)])


def summed(blocks):
    acc = blocks[0].astype(F32)
    for j in range(1, blocks.shape[0]):
        acc = acc + blocks[j].astype(F32)
    return acc


def sum_kernel(blocks, out):
    acc = summed(blocks).astype(out.dtype)
    for j in range(out.shape[0]):
        out[j] = acc


def sum_copies(blocks, count, dtype):
    (out,) = local(sum_kernel, [shape((count,) + blocks.shape[1:], dtype)], [blocks])
    return out


def total_kernel(blocks, out):
    out[...] = summed(blocks)


def query_kernel(w_query, latents_t, out):
    part = lax.dot_general(
        w_query[...], latents_t[...], (((0,), (0,)), ((), ())), preferred_element_type=F32
    )
    n, each, _ = out.shape
    for j in range(n):
        out[j] = part[j * each : (j + 1) * each]


def prepare_kernel(place, tokens, w_key, w_value, keys, keys_t, values, tokens_t, other_t, own_t):
    key = dot(tokens[...], w_key[...])
    keys[...] = key.astype(BF16)
    keys_t[...] = key.T.astype(BF16)
    values[...] = dot(tokens[...], w_value[...]).astype(BF16)
    for x in range(4):
        for w in range(4):
            at = (x * 4 + w) * 128
            slab = tokens[:, at : at + 128].T
            for y in range(4):
                tokens_t[x * 4 + y, w * 32 : (w + 1) * 32, :] = slab[y * 32 : (y + 1) * 32, :]
    z, c = place[2], place[3]
    hops, depth, cols = own_t.shape
    half = depth // 2
    for k in range(hops):
        for core, out in ((c, own_t), (1 - c, other_t)):
            rows = pl.ds(pl.multiple_of(((z ^ k) * 2 + core) * cols, cols), cols)
            out[k, :half, :] = w_key[rows, :].T
            out[k, half:, :] = w_value[rows, :].T


def expo_of(place, h, query_t, keys):
    rows, lats = keys.shape[0], query_t.shape[1]
    cols = slice(h * HEAD_DIM, (h + 1) * HEAD_DIM)
    pos_t = place[0] * rows + lax.broadcasted_iota(jnp.int32, (rows, lats), 0)
    pos_q = place[1] + lax.broadcasted_iota(jnp.int32, (rows, lats), 1)
    scores = dot(keys[:, cols], query_t[cols, :]) * SCALE
    return jnp.where(pos_t <= pos_q, jnp.exp(scores), 0.0)


def dprob_of(h, values, cot):
    cols = slice(h * HEAD_DIM, (h + 1) * HEAD_DIM)
    return dot_nt(values[:, cols], cot[:, cols])


def split(value):
    high = value.astype(BF16)
    return high, (value - high.astype(F32)).astype(BF16)


def dot_split(a, value):
    high, low = split(value)
    return dot(a, high) + dot(a, low)


def pack_sums(sums):
    high = sums.astype(BF16).astype(F32)
    middle = (sums - high).astype(BF16).astype(F32)
    low = sums - high - middle
    return jnp.concatenate([high, middle, low, jnp.zeros_like(sums)], axis=0).astype(BF16)


def unpack_sums(rows):
    rows = rows.astype(F32)
    return rows[0:4] + rows[4:8] + rows[8:12]


def mean_of(numer, denom):
    return jnp.where(denom > 0, numer / jnp.where(denom > 0, denom, 1.0), 0.0)


def mine_of(sums, place):
    first = place[4] < 8
    return jnp.where(first, sums[0:1], sums[2:3]), jnp.where(first, sums[1:2], sums[3:4])


def expo_kernel(place, query_t, keys, keys_t, values, cot, spread):
    heads = keys.shape[1] // HEAD_DIM
    n = spread.shape[0]
    each = keys.shape[1] // n
    per_head = n // heads
    sums = []
    for h in range(heads):
        cols = slice(h * HEAD_DIM, (h + 1) * HEAD_DIM)
        expo = expo_of(place, h, query_t, keys)
        weighted = expo * (dprob_of(h, values, cot) * SHRINK)
        denom = jnp.sum(expo, axis=0, keepdims=True)
        numer = jnp.sum(weighted, axis=0, keepdims=True)
        sums += [denom, numer]
        second = dot_split(keys_t[cols, :], expo)
        first = dot_split(keys_t[cols, :], weighted) - mean_of(numer, denom) * second
        first, second = first.astype(BF16), second.astype(BF16)
        for j in range(per_head):
            rows = slice(j * each, (j + 1) * each)
            spread[h * per_head + j, :each, :] = first[rows, :]
            spread[h * per_head + j, each : 2 * each, :] = second[rows, :]
    packed = pack_sums(jnp.concatenate(sums, axis=0))
    for j in range(n):
        spread[j, 2 * each :, :] = packed


def gathered(blocks, place):
    each = (blocks.shape[1] - 16) // 2
    sent = [unpack_sums(blocks[d, 2 * each :, :]) for d in range(blocks.shape[0])]
    sums = sent[0]
    for part in sent[1:]:
        sums = sums + part
    denom, numer = mine_of(sums, place)
    mean = mean_of(numer, denom)
    first = second = 0.0
    for d, part in enumerate(sent):
        denom_d, numer_d = mine_of(part, place)
        rows = blocks[d, each : 2 * each, :].astype(F32)
        first = first + blocks[d, :each, :].astype(F32) + (mean_of(numer_d, denom_d) - mean) * rows
        second = second + rows
    return sums, first, second


def sums_kernel(place, blocks, out):
    sums, first, second = gathered(blocks, place)
    each = first.shape[0]
    first, second, packed = first.astype(BF16), second.astype(BF16), pack_sums(sums)
    for j in range(out.shape[0]):
        out[j, :each, :] = first
        out[j, each : 2 * each, :] = second
        out[j, 2 * each :, :] = packed


def grad_kernel(
    place, sums4, query_t, keys, values, cot, tokens_hbm, other_hbm, blocks, both, other, tokens_t, other_t, sems
):
    fetch = pltpu.make_async_copy(tokens_hbm, tokens_t, sems.at[0])
    fetch_other = pltpu.make_async_copy(other_hbm, other_t, sems.at[1])
    fetch.start()
    fetch_other.start()
    heads = keys.shape[1] // HEAD_DIM
    sums, centred, _ = gathered(sums4, place)
    n, held, _ = blocks.shape
    depth = tokens_t.shape[1]
    each = held - depth
    for h in range(heads):
        cols = slice(h * HEAD_DIM, (h + 1) * HEAD_DIM)
        denom = sums[2 * h : 2 * h + 1, :]
        delta = sums[2 * h + 1 : 2 * h + 2, :] / denom * (1.0 / SHRINK)
        probs = expo_of(place, h, query_t, keys) / denom
        grad = (probs * (dprob_of(h, values, cot) - delta) * SCALE).astype(BF16)
        both[:, cols] = dot_nt(grad, query_t[cols, :]).astype(BF16)
        value_cols = slice((heads + h) * HEAD_DIM, (heads + h + 1) * HEAD_DIM)
        both[:, value_cols] = dot(probs.astype(BF16), cot[:, cols]).astype(BF16)
    query_grad = (centred / mine_of(sums, place)[0] * (SCALE / SHRINK)).astype(BF16)
    fetch.wait()
    tall = 4
    for j in range(0, n, tall):
        part = dot(tokens_t[j : j + tall].reshape(tall * depth, -1), both[...]).astype(BF16)
        for i in range(tall):
            blocks[j + i, :depth, :] = part[i * depth : (i + 1) * depth]
            blocks[j + i, depth:, :] = query_grad
    fetch_other.wait()
    for k in range(other.shape[0]):
        other[k] = dot(both[...], other_t[k]).astype(BF16)


def pair_kernel(both, weights, other, here, *away):
    here[...] = dot(both[...], weights[0]) + other[0].astype(F32)
    for k, out in enumerate(away):
        out[...] = (dot(both[...], weights[k + 1]) + other[k + 1].astype(F32)).astype(BF16)


def token_sum_kernel(here, one, two, three, out):
    total = here[...] + one[...].astype(F32) + two[...].astype(F32) + three[...].astype(F32)
    out[...] = total.astype(BF16)


def latent_sum_kernel(place, own, two, three, one, out, terms):
    for k, term in enumerate((own, one, two, three)):
        terms[k] = term[...].astype(F32)
    z = place[2]
    out[...] = ((terms[z] + terms[z ^ 1]) + terms[z ^ 2]) + terms[z ^ 3]


def near_sum_kernel(arrived, w_query, latents_t, out, latent, query_weight):
    far, share, _ = out.shape
    depth = far * share
    n, held, lats = arrived.shape
    acc = arrived[0, :depth, :].astype(F32)
    for j in range(1, n):
        acc = acc + arrived[j, :depth, :].astype(F32)
    for w in range(far):
        out[w] = acc[w * share : (w + 1) * share].astype(BF16)
    query_grad_t = arrived[:, depth:, :].reshape(n * (held - depth), lats)
    latent[...] = dot(w_query[...], query_grad_t).astype(BF16)
    query_weight[...] = dot_nt(latents_t[...], query_grad_t)


def far_sum_kernel(arrived, key_weight, value_weight):
    width = key_weight.shape[1]
    acc = summed(arrived)
    key_weight[...] = acc[:, :width]
    value_weight[...] = acc[:, width:]


def on_device(tokens, latents, w_query, w_key, w_value, cotangent):
    rows, depth = tokens.shape
    lats = latents.shape[0]
    width = w_key.shape[1]
    heads = width // HEAD_DIM
    near, far = lax.axis_size(NEAR), lax.axis_size("w")
    n_seq = lax.axis_size(SEQ)
    n_head = lax.axis_size(HEAD)
    share = depth // n_seq
    each = width // near
    z, c = lax.axis_index("z"), lax.axis_index("c")
    place = jnp.stack([lax.axis_index(SEQ), rows * n_seq - lats, z, c, lax.axis_index(NEAR)])
    place = place.astype(jnp.int32)
    scalars = {0: SMEM}

    (query_part,) = local(
        query_kernel, [shape((near, each, lats), F32)], [w_query, latents.T], 2 * share * width * lats, limit=60
    )
    query_part = exchange(query_part, NEAR)
    block = depth // n_head
    hops = n_head // 2
    keys, keys_t, values, tokens_t, other_t, own_t = local(
        prepare_kernel,
        [
            shape((rows, width), BF16),
            shape((width, rows), BF16),
            shape((rows, width), BF16),
            shape((near, depth // near, rows), BF16),
            shape((hops, 2 * width, block), BF16),
            shape((hops, 2 * width, block), BF16),
        ],
        [place, tokens, w_key, w_value],
        2 * rows * depth * 2 * width,
        specs=scalars,
        limit=60,
    )

    query_part = exchange(sum_copies(query_part, far, F32), "w")
    query_part, keys, keys_t, values, tokens_t, other_t, own_t = lax.optimization_barrier(
        (query_part, keys, keys_t, values, tokens_t, other_t, own_t)
    )
    query_t = exchange(sum_copies(query_part, near, BF16), NEAR).reshape(width, lats)

    (spread,) = local(
        expo_kernel,
        [shape((near, 2 * each + 16, lats), BF16)],
        [place, query_t, keys, keys_t, values, cotangent],
        12 * rows * width * lats,
        specs=scalars,
        limit=60,
    )
    (spread,) = local(
        sums_kernel,
        [shape((far,) + spread.shape[1:], BF16)],
        [place, exchange(spread, NEAR)],
        specs=scalars,
    )
    sums = exchange(spread, "w")

    blocks, both, other = local(
        grad_kernel,
        [
            shape((near, depth // near + each, 2 * width), BF16),
            shape((rows, 2 * width), BF16),
            shape((hops, rows, block), BF16),
        ],
        [place, sums, query_t, keys, values, cotangent, tokens_t, other_t],
        8 * rows * width * lats + 3 * rows * depth * 2 * width,
        specs={0: SMEM, 6: HBM, 7: HBM},
        scratch=[
            pltpu.VMEM(tokens_t.shape, BF16),
            pltpu.VMEM(other_t.shape, BF16),
            pltpu.SemaphoreType.DMA((2,)),
        ],
        limit=60,
    )
    arrived = exchange(blocks, NEAR)

    here, *away = local(
        pair_kernel,
        [shape((rows, block), F32)] + [shape((rows, block), BF16)] * (hops - 1),
        [both, own_t, partner(other, "c", 1)],
        rows * depth * 2 * width,
        limit=60,
    )
    parts = [partner(away[k - 1], "z", k) for k in (2, 3, 1)]
    arrived, here, *parts = lax.optimization_barrier((arrived, here, *parts))
    (token_grad,) = local(token_sum_kernel, [shape((rows, block), BF16)], [here, *parts], limit=60)

    sent, held, query_weight_grad = local(
        near_sum_kernel,
        [
            shape((far, share, 2 * width), BF16),
            shape((share, lats), BF16),
            shape((share, width), F32),
        ],
        [arrived, w_query, latents.T],
        4 * share * width * lats,
    )
    key_weight_grad, value_weight_grad = local(
        far_sum_kernel, [shape((share, width), F32)] * 2, [exchange(sent, "w")]
    )
    held = (held.astype(F32) + partner(held, "c", 1).astype(F32)).astype(BF16)
    (latent_grad_t,) = local(
        latent_sum_kernel,
        [shape((share, lats), F32)],
        [place, held] + [partner(held, "z", k) for k in (2, 3, 1)],
        specs=scalars,
        scratch=[pltpu.VMEM((hops, share, lats), F32)],
    )
    return (
        token_grad,
        latent_grad_t.T,
        query_weight_grad,
        key_weight_grad,
        value_weight_grad,
    )


def solution(mesh):
    fine = Mesh(mesh.devices.reshape(4, 4, 4, 4, 2), ("x", "w", "y", "z", "c"))
    placed = (
        P(SEQ, None),
        P(None, SEQ),
        P(SEQ, HEAD),
        P(None, HEAD),
        P(None, HEAD),
        P(None, HEAD),
    )
    return jax.shard_map(
        on_device,
        mesh=fine,
        in_specs=placed,
        out_specs=(
            P(SEQ, HEAD),
            P(None, SEQ),
            P(SEQ, HEAD),
            P(SEQ, HEAD),
            P(SEQ, HEAD),
        ),
        check_vma=False,
    )
```
